128 devices in a mesh: ch: 32 (over x, y, z_hi), half: 4 (over z_lo, core).
Axes of the slice: x: 4, y: 4, z: 4 (z_hi: 2, z_lo: 2; z = z_hi * 2 + z_lo), core: 2. Of those that a mesh axis runs over, the one named last changes fastest.
Arguments:
- pair_act: bfloat16 [768, 768, 128], P('half', 'ch'), may hold values from -6 to 6
- tri_out: bfloat16 [768, 768, 128], P('half', 'ch'), may hold values from -48 to 48
- cotangent: bfloat16 [768, 768, 128], P('half', 'ch'), may hold values from -6 to 6
- residue_mask: int32 [768], replicated, may hold values 0 or 1
- chain_index: int32 [768], replicated, may hold values from 0 to 3, never falling along the last dimension, each value on 1 to 384 neighbouring positions
- chain_pairs: int32 [4, 4], replicated, may hold values 0 or 1
- in_weight: bfloat16 [128, 640], replicated, may hold values from -0.5 to 0.5
- out_weight: bfloat16 [128, 128], replicated, may hold values from -0.5 to 0.5
- in_gain: float32 [128], replicated, may hold values from 0.1 to 1.9
- in_bias: float32 [128], replicated, may hold values from -3 to 3
- out_gain: float32 [128], replicated, may hold values from 0.1 to 1.9
- out_bias: float32 [128], replicated, may hold values from -3 to 3
Outputs:
- grad_pair: bfloat16 [768, 768, 128], P('half', 'ch')
The draws below stay inside these ranges and needn't reach their ends.
Inputs may be any that keep to these rules, and one draw needn't show every extreme that they name: `chain_index`: chains are numbered in order along the residues, never falling; one chain has 384 residues.
All inputs are finite; a program needn't handle non-finite values.
Results may differ from the reference program's by a relative error of at most 0.015.
Values may be sent and summed in bfloat16 or wider, within the bound.
No kernel may reach another device: no remote copies, remote signals or barrier semaphores. Data moves between devices by JAX's collectives and lax.ppermute only.
A program may use at most 128 MiB of HBM per device.

```python
import math
import jax
import jax.numpy as jnp
import numpy as np
from jax import lax

C = 128
RES = 768
CHAINS = 4


def touch_ends(result, rng, low, high):
    longest = result.shape.index(max(result.shape))
    spots = []
    for shift in (0, 1):
        where = [jax.random.randint(jax.random.fold_in(rng, axis), (), 0, length) for axis, length in enumerate(result.shape)]
        where[longest] = (where[longest] + shift) % result.shape[longest]
        spots.append(tuple(where))
    return result.at[spots[0]].set(low).at[spots[1]].set(high)


def block_levels(stream_key, shape, pieces, least, largest):
    level = 1.0
    for axis_at, parts in pieces:
        draws = jax.random.uniform(jax.random.fold_in(jax.random.fold_in(stream_key, 6), axis_at), (parts,), jnp.float32, least / len(pieces), largest / len(pieces))
        level = level * jnp.repeat(jnp.exp(draws), shape[axis_at] // parts).reshape((-1,) + (1,) * (len(shape) - 1 - axis_at))
    return level


def length_profile(amount, total, reach, slope):
    loads = [(1 << 20) // math.isqrt(standing ** slope) + 1 for standing in range(2, amount + 1)]
    surplus, given = total - reach - (amount - 1), [1] * (amount - 1)
    while surplus > 0:
        free = [i for i in range(amount - 1) if given[i] < reach]
        whole, remaining = sum([loads[i] for i in free]), surplus
        for i in free:
            extra = min(reach - given[i], max(1, remaining * loads[i] // whole), surplus)
            given[i] = given[i] + extra
            surplus = surplus - extra
    return np.array([reach] + given)


def ragged_sizes(rng, count, total, limit, slope):
    if count == 2:
        one = jax.random.randint(rng, (), max(1, total - limit), min(limit, total - 1) + 1)
        return jnp.stack([one, total - one])
    tallies = jnp.asarray(length_profile(count, total, limit, slope), jnp.int32)
    pairs = (count - 1) // 2
    giver, receiver = tallies[1:1 + 2 * pairs:2], tallies[2:2 + 2 * pairs:2]
    slack = jnp.minimum(giver - 1, limit - receiver)
    moved = jax.random.randint(jax.random.fold_in(rng, 1), (pairs,), 0, 1 << 20) % (slack + 1)
    tallies = tallies.at[1:1 + 2 * pairs:2].set(giver - moved).at[2:2 + 2 * pairs:2].set(receiver + moved)
    return tallies[jax.random.permutation(jax.random.fold_in(rng, 2), count)]


def gaussian(rng, shape, width, reach, split=(), kind=jnp.bfloat16):
    array = jax.random.normal(rng, shape, jnp.float32) * width
    if len(split) > 0:
        array = block_levels(rng, shape, split, -0.22, 0.18) * array
    return jnp.clip(array, min=-reach, max=reach).astype(kind)


def setup_inputs(seed: int = 0) -> dict:
    splits = jax.random.split(jax.random.key(seed), 13)
    pair_act = gaussian(splits[0], (RES, RES, C), 1.0, 6.0, ((0, 4), (1, 32)))
    tri_out = gaussian(splits[1], (RES, RES, C), 8.0, 48.0, ((0, 4), (1, 32)))
    cotangent = gaussian(splits[2], (RES, RES, C), 1.0, 6.0, ((0, 4), (1, 32)))
    residue_mask = touch_ends((jax.random.randint(splits[3], (RES,), 0, 16) < 15).astype(jnp.int32), jax.random.fold_in(splits[3], 1), 0, 1)
    chain_index = jnp.searchsorted(jnp.cumsum(ragged_sizes(splits[4], CHAINS, RES, RES // 2, 2)), jnp.arange(RES), side="right").astype(jnp.int32)
    chain_pairs = touch_ends((jax.random.randint(splits[5], (CHAINS, CHAINS), 0, 4) < 3).astype(jnp.int32), jax.random.fold_in(splits[5], 1), 0, 1)
    in_weight = gaussian(splits[6], (C, 5 * C), C ** -0.5, 0.5)
    out_weight = gaussian(splits[7], (C, C), C ** -0.5, 0.5)
    in_gain = jnp.clip(1.0 + 0.18 * jax.random.normal(splits[8], (C,), jnp.float32), 0.1, 1.9)
    in_bias = gaussian(splits[9], (C,), 0.5, 3.0, (), jnp.float32)
    out_gain = jnp.clip(1.0 + 0.18 * jax.random.normal(splits[10], (C,), jnp.float32), 0.1, 1.9)
    out_bias = gaussian(splits[11], (C,), 0.5, 3.0, (), jnp.float32)
    return {"pair_act": pair_act, "tri_out": tri_out, "cotangent": cotangent, "residue_mask": residue_mask, "chain_index": chain_index, "chain_pairs": chain_pairs, "in_weight": in_weight, "out_weight": out_weight, "in_gain": in_gain, "in_bias": in_bias, "out_gain": out_gain, "out_bias": out_bias}


EPSILON = 1e-05

def normalize(values, gain, bias):
    centre = lax.optimization_barrier(jnp.mean(values, -1, keepdims=True))
    centred = values - centre
    inv_scale = lax.rsqrt(lax.optimization_barrier(jnp.mean(centred * centred, -1, keepdims=True)) + EPSILON)
    unit_val = centred * inv_scale
    return (unit_val * gain + bias, unit_val, inv_scale)

def norm_back(grad_in, unit_val, inv_scale):
    first_mean = lax.optimization_barrier(jnp.mean(grad_in, -1, keepdims=True))
    second_mean = lax.optimization_barrier(jnp.mean(grad_in * unit_val, -1, keepdims=True))
    return inv_scale * (grad_in - first_mean - unit_val * second_mean)

def pair_keep(residue_mask, chain_index, chain_pairs):
    labels = jnp.arange(chain_pairs.shape[0], dtype=jnp.int32)
    onehot = (chain_index[:, None] == labels[None, :]).astype(jnp.float32)
    allowed = jnp.dot(jnp.dot(onehot, chain_pairs.astype(jnp.float32)), onehot.T)
    keep_res = residue_mask.astype(jnp.float32)
    return allowed * keep_res[:, None] * keep_res[None, :]

def to_wide(narrow):
    return lax.optimization_barrier(narrow).astype(jnp.float32)

def recompute(pair_rows, tri_rows, cot_rows, keep_rows, in_weight, out_weight, in_gain, in_bias, out_gain, out_bias):
    channels = pair_rows.shape[-1]
    normed, unit_z, inv_z = normalize(pair_rows.astype(jnp.float32), in_gain, in_bias)
    normed_b = to_wide(normed.astype(jnp.bfloat16))
    projected = jnp.einsum('ikd,de->ike', normed_b, in_weight.astype(jnp.float32))
    left_proj = projected[..., :channels]
    left_gate = jax.nn.sigmoid(projected[..., channels:2 * channels])
    right_proj = projected[..., 2 * channels:3 * channels]
    right_gate = jax.nn.sigmoid(projected[..., 3 * channels:4 * channels])
    out_gate = jax.nn.sigmoid(projected[..., 4 * channels:])
    keep_col = keep_rows[:, :, None]
    left = (keep_col * left_gate * left_proj).astype(jnp.bfloat16)
    right = (keep_col * right_gate * right_proj).astype(jnp.bfloat16)
    normed_x, unit_x, inv_x = normalize(tri_rows.astype(jnp.float32), out_gain, out_bias)
    normed_xb = to_wide(normed_x.astype(jnp.bfloat16))
    out_proj = jnp.einsum('ikc,cd->ikd', normed_xb, out_weight.astype(jnp.float32))
    grad_outer = to_wide((cot_rows * out_gate).astype(jnp.bfloat16))
    grad_normed = jnp.einsum('ikd,cd->ikc', grad_outer, out_weight.astype(jnp.float32))
    grad_tri = norm_back(grad_normed * out_gain, unit_x, inv_x).astype(jnp.bfloat16)
    grad_gate = cot_rows * out_proj
    saved = (left_proj, left_gate, right_proj, right_gate, out_gate, grad_gate, unit_z, inv_z)
    return (left, right, grad_tri, saved)

def reference(pair_act, tri_out, cotangent, residue_mask, chain_index, chain_pairs, in_weight, out_weight, in_gain, in_bias, out_gain, out_bias):
    keep = pair_keep(residue_mask, chain_index, chain_pairs)
    blocks = RES // 64

    def in_blocks(values):
        return values.reshape((blocks, 64) + values.shape[1:])

    def first_pass(inputs):
        pair_rows, tri_rows, cot_rows, keep_rows = inputs
        left, right, grad_tri, saved = recompute(pair_rows, tri_rows, cot_rows, keep_rows, in_weight, out_weight, in_gain, in_bias, out_gain, out_bias)
        return (left, right, grad_tri)
    left, right, grad_tri = lax.map(first_pass, (in_blocks(pair_act), in_blocks(tri_out), in_blocks(cotangent), in_blocks(keep)))
    full_shape = (RES, RES, C)
    left_c = jnp.transpose(left.reshape(full_shape), (2, 0, 1))
    right_c = jnp.transpose(right.reshape(full_shape), (2, 0, 1))
    grad_c = jnp.transpose(grad_tri.reshape(full_shape), (2, 0, 1))

    def channel(inputs):
        left_m, right_m, grad_m = inputs
        grad_l = jnp.dot(grad_m, right_m, preferred_element_type=jnp.float32).astype(jnp.bfloat16)
        grad_r = jnp.dot(grad_m.T, left_m, preferred_element_type=jnp.float32).astype(jnp.bfloat16)
        return (grad_l, grad_r)
    grad_left_c, grad_right_c = lax.map(channel, (left_c, right_c, grad_c))
    grad_left = jnp.transpose(grad_left_c, (1, 2, 0))
    grad_right = jnp.transpose(grad_right_c, (1, 2, 0))

    def second_pass(inputs):
        pair_rows, tri_rows, cot_rows, keep_rows, gl_rows, gr_rows = inputs
        left, right, grad_tri, saved = recompute(pair_rows, tri_rows, cot_rows, keep_rows, in_weight, out_weight, in_gain, in_bias, out_gain, out_bias)
        left_proj, left_gate, right_proj, right_gate, out_gate, grad_gate, unit_z, inv_z = saved
        keep_col = keep_rows[:, :, None]
        grad_l = gl_rows.astype(jnp.float32) * keep_col
        grad_r = gr_rows.astype(jnp.float32) * keep_col
        grad_proj = jnp.concatenate([grad_l * left_gate, grad_l * left_proj * left_gate * (1.0 - left_gate), grad_r * right_gate, grad_r * right_proj * right_gate * (1.0 - right_gate), grad_gate * out_gate * (1.0 - out_gate)], -1)
        grad_proj = to_wide(grad_proj.astype(jnp.bfloat16))
        grad_normed = jnp.einsum('ike,de->ikd', grad_proj, in_weight.astype(jnp.float32))
        return norm_back(grad_normed * in_gain, unit_z, inv_z).astype(jnp.bfloat16)
    grad_pair = lax.map(second_pass, (in_blocks(pair_act), in_blocks(tri_out), in_blocks(cotangent), in_blocks(keep), in_blocks(grad_left), in_blocks(grad_right)))
    return grad_pair.reshape(full_shape)
```

```python
import functools

import jax
import jax.numpy as jnp
from jax import lax
from jax.experimental import pallas as pl
from jax.experimental.pallas import tpu as pltpu
from jax.sharding import PartitionSpec as P

EPSILON = 1e-05
AXES = ("ch", "half")
F32 = jnp.float32
BF16 = jnp.bfloat16

ROWS, COLS, C = 192, 24, 128
HALF_COLS = COLS // 2
OUT_ROWS = 112
BACK_ROWS = 72
G_A, G_B, L_A, R_A, LR_B = 0, 24, 40, 64, 88
RES = 768


def dot(a, b):
    return jnp.dot(a, b, preferred_element_type=F32)


def sigmoid(x):
    return 0.5 * jnp.tanh(0.5 * x) + 0.5


def unit(x):
    centred = x - jnp.mean(x, 0, keepdims=True)
    inv = lax.rsqrt(jnp.mean(centred * centred, 0, keepdims=True) + EPSILON)
    return centred * inv, inv


def norm_back(grad, unit_val, inv):
    first = jnp.mean(grad, 0, keepdims=True)
    second = jnp.mean(grad * unit_val, 0, keepdims=True)
    return inv * (grad - first - unit_val * second)


def tile3(x):
    return jnp.concatenate([x, x, x], 1)


def column(row):
    return jnp.broadcast_to(row, (C, C)).T


def swap(x):
    return pltpu.roll(x, 64, 1)


def low_lanes(shape):
    return lax.broadcasted_iota(jnp.int32, shape, 1) < 64


def spread(src, dst):
    def body(i, _):
        at = pl.multiple_of(i * 8, 8)
        dst[pl.ds(pl.multiple_of(i * 192, 8), 192), :] = src[pl.ds(at, 8)].astype(F32).reshape(192, C)
        return 0

    lax.fori_loop(0, ROWS // 8, body, 0)


def gather_cols(src, q):
    base = C * COLS
    parts = [
        src[pl.ds(q, C, stride=COLS), :],
        src[pl.ds(q + HALF_COLS, C, stride=COLS), :],
        src[pl.ds(base + q, 64, stride=COLS), :],
        src[pl.ds(base + q + HALF_COLS, 64, stride=COLS), :],
    ]
    return jnp.concatenate(parts, 0).T


def row_code(mask_ref, chain_ref):
    half = lax.axis_index("half")
    code = jnp.where(mask_ref[...] > 0, chain_ref[...], -1)
    code = jnp.broadcast_to(code, (8, RES))
    code = pltpu.roll(code, lax.rem(RES - half * ROWS, RES), 1)[:1]
    low = code[:, C : C + C]
    return code[:, :C], jnp.where(low_lanes((1, C)), low, swap(low))


def keep_row(q, codes, mask_s, chain_s, pairs_s):
    first = lax.axis_index("ch") * COLS + q
    factors = []
    for k in (first, first + HALF_COLS):
        chain = chain_s[k]
        factors.append([(pairs_s[c, chain] * mask_s[k]).astype(F32) for c in range(4)])

    def pick(code, factor):
        out = jnp.zeros(code.shape, F32)
        for c in range(4):
            out = jnp.where(code == c, factor[c], out)
        return out

    code_a, code_b = codes
    tail = jnp.where(low_lanes((1, C)), pick(code_b, factors[0]), pick(code_b, factors[1]))
    return jnp.concatenate([pick(code_a, factors[0]), pick(code_a, factors[1]), tail], 1)


def prepare(w_ref, wo_ref, gains, wt, wot, cols):
    wt[...] = w_ref[...].astype(F32).T.astype(BF16)
    wot[...] = wo_ref[...].astype(F32).T.astype(BF16)
    for n, g in enumerate(gains):
        cols[n] = column(g[...])


def front_kernel(
    pair_ref, tri_ref, cot_ref, mask_v, chain_v, mask_s, chain_s, pairs_s,
    w_ref, wo_ref, in_gain, in_bias, out_gain, out_bias, out_ref,
    xp, xt, xc, wt, wot, cols, stage,
):
    prepare(w_ref, wo_ref, (in_gain, in_bias, out_gain, out_bias), wt, wot, cols)
    spread(pair_ref, xp)
    spread(tri_ref, xt)
    spread(cot_ref, xc)
    codes = row_code(mask_v, chain_v)

    def put(row, value):
        stage[pl.ds(row, C, stride=OUT_ROWS), :] = value

    for r in range(4):
        put(36 + r, jnp.zeros((C, C), F32))

    def body(q, _):
        keep = keep_row(q, codes, mask_s, chain_s, pairs_s)
        z, _ = unit(gather_cols(xp, q))
        nz = (z * tile3(cols[0]) + tile3(cols[1])).astype(BF16)
        proj = dot(wt[...], nz)
        left = keep * sigmoid(proj[C : 2 * C]) * proj[:C]
        right = keep * sigmoid(proj[3 * C : 4 * C]) * proj[2 * C : 3 * C]
        outer = (gather_cols(xc, q) * sigmoid(proj[4 * C :])).astype(BF16)
        u, inv = unit(gather_cols(xt, q))
        grad = norm_back(dot(wo_ref[...], outer) * tile3(cols[2]), u, inv)
        put(G_A + q, grad[:, :C])
        put(G_A + HALF_COLS + q, grad[:, C : 2 * C])
        put(G_B + q, grad[:, 2 * C :])
        put(L_A + q, left[:, :C])
        put(L_A + HALF_COLS + q, left[:, C : 2 * C])
        put(R_A + q, right[:, :C])
        put(R_A + HALF_COLS + q, right[:, C : 2 * C])
        low = low_lanes((C, C))
        tail_l, tail_r = left[:, 2 * C :], right[:, 2 * C :]
        put(LR_B + q, jnp.where(low, tail_l, swap(tail_r)))
        put(LR_B + HALF_COLS + q, jnp.where(low, swap(tail_l), tail_r))
        return 0

    lax.fori_loop(0, HALF_COLS, body, 0)

    def flush(c, _):
        at = pl.multiple_of(c * OUT_ROWS, 8)
        out_ref[c] = stage[pl.ds(at, OUT_ROWS), :].astype(BF16)
        return 0

    lax.fori_loop(0, C, flush, 0)


def save_kernel(
    pair_ref, tri_ref, cot_ref, mask_v, chain_v, mask_s, chain_s, pairs_s,
    w_ref, wo_ref, in_gain, in_bias, out_gain, out_bias, saved_ref, inv_ref,
    xp, xt, xc, wt, wot, cols,
):
    prepare(w_ref, wo_ref, (in_gain, in_bias, out_gain, out_bias), wt, wot, cols)
    spread(pair_ref, xp)
    spread(tri_ref, xt)
    spread(cot_ref, xc)
    codes = row_code(mask_v, chain_v)

    def body(q, _):
        keep = keep_row(q, codes, mask_s, chain_s, pairs_s)
        z, inv_z = unit(gather_cols(xp, q))
        nz = (z * tile3(cols[0]) + tile3(cols[1])).astype(BF16)
        proj = dot(wt[...], nz)
        gate_l = sigmoid(proj[C : 2 * C])
        gate_r = sigmoid(proj[3 * C : 4 * C])
        gate_o = sigmoid(proj[4 * C :])
        u, _ = unit(gather_cols(xt, q))
        nx = (u * tile3(cols[2]) + tile3(cols[3])).astype(BF16)
        out_proj = dot(wot[...], nx)
        keep_l, keep_r = keep * gate_l, keep * gate_r
        saved_ref[q, 0] = keep_l.astype(BF16)
        saved_ref[q, 1] = (keep_l * proj[:C] * (1.0 - gate_l)).astype(BF16)
        saved_ref[q, 2] = keep_r.astype(BF16)
        saved_ref[q, 3] = (keep_r * proj[2 * C : 3 * C] * (1.0 - gate_r)).astype(BF16)
        saved_ref[q, 4] = (gather_cols(xc, q) * out_proj * gate_o * (1.0 - gate_o)).astype(BF16)
        saved_ref[q, 5] = z.astype(BF16)
        inv_ref[q] = jnp.broadcast_to(inv_z, (8, 3 * C))
        return 0

    lax.fori_loop(0, HALF_COLS, body, 0)


def channel_kernel(in_ref, out_ref, g, left, right, back_l, back_r):
    low24 = low_lanes((COLS, C))
    low12 = low_lanes((HALF_COLS, C))

    def take(w):
        blocks = [in_ref[w * 4 + h].astype(F32) for h in range(4)]
        rows_g = [b[G_A : G_A + COLS] for b in blocks]
        rows_l = [b[L_A : L_A + COLS] for b in blocks]
        rows_r = [b[R_A : R_A + COLS] for b in blocks]
        for h in (0, 2):
            a, b = blocks[h][G_B : G_B + HALF_COLS], blocks[h + 1][G_B : G_B + HALF_COLS]
            rows_g.append(jnp.concatenate([jnp.where(low12, a, swap(b)), jnp.where(low12, swap(a), b)], 0))
            a, b = blocks[h][LR_B : LR_B + COLS], blocks[h + 1][LR_B : LR_B + COLS]
            rows_l.append(jnp.where(low24, a, swap(b)))
            rows_r.append(jnp.where(low24, swap(a), b))
        return [jnp.concatenate(rows, 1) for rows in (rows_g, rows_l, rows_r)]

    def gather(pair, _):
        one, two = take(2 * pair), take(2 * pair + 1)
        at = pl.ds(pl.multiple_of(pair * 48, 16), 48)
        for ref, a, b in zip((g, left, right), one, two):
            ref[at, :] = jnp.concatenate([a, b], 0).astype(BF16)
        return 0

    lax.fori_loop(0, 16, gather, 0)
    spans = [(ROWS * h, C) for h in range(4)] + [(ROWS * h + C, 64) for h in range(4)]
    ordered = jnp.concatenate([g[at : at + size, :] for at, size in spans], 0)
    back_l[...] = dot(right[...], ordered)
    back_r[...] = lax.dot_general(left[...], ordered, (((1,), (1,)), ((), ())), preferred_element_type=F32)

    def give(w, _):
        at = pl.ds(pl.multiple_of(w * COLS, 8), COLS)
        for h in range(4):
            lanes = slice(h * C, (h + 1) * C)
            tail = slice((4 + h // 2) * C, (5 + h // 2) * C)
            a, b = back_l[at, tail], back_r[at, tail]
            mixed = jnp.where(low24, a, swap(b)) if h % 2 == 0 else jnp.where(low24, swap(a), b)
            out_ref[w * 4 + h] = jnp.concatenate([back_l[at, lanes], back_r[at, lanes], mixed], 0).astype(BF16)
        return 0

    lax.fori_loop(0, 32, give, 0)


def back_kernel(in_ref, saved_ref, inv_ref, w_ref, in_gain, out_ref, rows, cols, stage):
    cols[...] = column(in_gain[...])

    def fill(c, _):
        at = pl.multiple_of(c * BACK_ROWS, 8)
        rows[pl.ds(at, BACK_ROWS), :] = in_ref[c].astype(F32)
        return 0

    lax.fori_loop(0, C, fill, 0)

    def body(q, _):
        low = low_lanes((C, C))

        def get(row):
            return rows[pl.ds(row, C, stride=BACK_ROWS), :]

        a, b = get(48 + q), get(48 + HALF_COLS + q)
        tail_l = jnp.where(low, a, swap(b))
        tail_r = jnp.where(low, swap(a), b)
        grad_l = jnp.concatenate([get(q), get(HALF_COLS + q), tail_l], 1)
        grad_r = jnp.concatenate([get(COLS + q), get(COLS + HALF_COLS + q), tail_r], 1)
        grad_proj = jnp.concatenate(
            [
                (grad_l * saved_ref[q, 0].astype(F32)).astype(BF16),
                (grad_l * saved_ref[q, 1].astype(F32)).astype(BF16),
                (grad_r * saved_ref[q, 2].astype(F32)).astype(BF16),
                (grad_r * saved_ref[q, 3].astype(F32)).astype(BF16),
                saved_ref[q, 4],
            ],
            0,
        )
        e = dot(w_ref[...], grad_proj) * tile3(cols[...])
        grad = norm_back(e, saved_ref[q, 5].astype(F32), inv_ref[q][:1]).T
        base = C * COLS
        stage[pl.ds(q, C, stride=COLS), :] = grad[:C]
        stage[pl.ds(q + HALF_COLS, C, stride=COLS), :] = grad[C : 2 * C]
        stage[pl.ds(base + q, 64, stride=COLS), :] = grad[2 * C : 2 * C + 64]
        stage[pl.ds(base + q + HALF_COLS, 64, stride=COLS), :] = grad[2 * C + 64 :]
        return 0

    lax.fori_loop(0, HALF_COLS, body, 0)

    def flush(i, _):
        at = pl.multiple_of(i * 8, 8)
        rows8 = stage[pl.ds(pl.multiple_of(i * 192, 8), 192), :].reshape(8, COLS, C)
        out_ref[pl.ds(at, 8)] = rows8.astype(BF16)
        return 0

    lax.fori_loop(0, ROWS // 8, flush, 0)


def call(kernel, outs, scratch, args, smem=(), flops=0, moved=0, limit=30):
    vmem, scal = pl.BlockSpec(memory_space=pltpu.VMEM), pl.BlockSpec(memory_space=pltpu.SMEM)
    single = not isinstance(outs, tuple)
    return pl.pallas_call(
        kernel,
        out_shape=outs,
        in_specs=[scal if n in smem else vmem for n in range(len(args))],
        out_specs=vmem if single else tuple(vmem for _ in outs),
        scratch_shapes=scratch,
        compiler_params=pltpu.CompilerParams(vmem_limit_bytes=limit << 20),
        cost_estimate=pl.CostEstimate(flops=flops, bytes_accessed=moved, transcendentals=0),
    )(*args)


def exchange(x):
    return lax.all_to_all(x, AXES, split_axis=0, concat_axis=0, tiled=True)


def on_device(
    pair_act,
    tri_out,
    cotangent,
    residue_mask,
    chain_index,
    chain_pairs,
    in_weight,
    out_weight,
    in_gain,
    in_bias,
    out_gain,
    out_bias,
):
    shape = jax.ShapeDtypeStruct
    gains = [g.reshape(1, C) for g in (in_gain, in_bias, out_gain, out_bias)]
    given = [
        pair_act, tri_out, cotangent, residue_mask.reshape(1, RES), chain_index.reshape(1, RES),
        residue_mask, chain_index, chain_pairs, in_weight, out_weight, *gains,
    ]
    smem = (5, 6, 7)
    tile = pltpu.VMEM((ROWS * COLS, C), F32)
    shared = [tile, tile, tile, pltpu.VMEM((5 * C, C), BF16), pltpu.VMEM((C, C), BF16), pltpu.VMEM((4, C, C), F32)]
    sent = call(
        front_kernel,
        shape((C, OUT_ROWS, C), BF16),
        shared + [pltpu.VMEM((C * OUT_ROWS, C), F32)],
        given,
        smem,
        flops=2 * 4608 * 128 * 768,
        moved=8 << 20,
    )
    saved, inv = call(
        save_kernel,
        (shape((HALF_COLS, 6, C, 3 * C), BF16), shape((HALF_COLS, 8, 3 * C), F32)),
        shared,
        given,
        smem,
        flops=2 * 4608 * 128 * 768,
        moved=12 << 20,
    )
    got = exchange(sent)
    square = pltpu.VMEM((RES, RES), BF16)
    wide = pltpu.VMEM((RES, RES), F32)
    back = call(
        channel_kernel,
        shape((C, BACK_ROWS, C), BF16),
        [square, square, square, wide, wide],
        [got],
        flops=4 * RES**3,
        moved=8 << 20,
    )
    returned = exchange(back)
    return call(
        back_kernel,
        shape((ROWS, COLS, C), BF16),
        [pltpu.VMEM((C * BACK_ROWS, C), F32), pltpu.VMEM((C, C), F32), tile],
        [returned, saved, inv, in_weight, gains[0]],
        flops=2 * 4608 * 128 * 640,
        moved=12 << 20,
    )


def solution(mesh):
    return jax.shard_map(
        on_device,
        mesh=mesh,
        in_specs=(P("half", "ch", None),) * 3 + (P(),) * 9,
        out_specs=P("half", "ch", None),
        check_vma=False,
    )
```

```python
import functools

import jax
import jax.numpy as jnp
from jax import lax
from jax.experimental import pallas as pl
from jax.experimental.pallas import tpu as pltpu
from jax.sharding import PartitionSpec as P

EPSILON = 1e-05
AXES = ("ch", "half")
F32 = jnp.float32
BF16 = jnp.bfloat16

ROWS, COLS, C = 192, 24, 128
HALF_COLS = COLS // 2
OUT_ROWS = 112
BACK_ROWS = 72
G_A, G_B, L_A, R_A, LR_B = 0, 24, 40, 64, 88
RES = 768


def dot(a, b):
    return jnp.dot(a, b, preferred_element_type=F32)


def sigmoid(x):
    return 0.5 * jnp.tanh(0.5 * x) + 0.5


def unit(x):
    centred = x - jnp.mean(x, 0, keepdims=True)
    inv = lax.rsqrt(jnp.mean(centred * centred, 0, keepdims=True) + EPSILON)
    return centred * inv, inv


def norm_back(grad, unit_val, inv):
    first = jnp.mean(grad, 0, keepdims=True)
    second = jnp.mean(grad * unit_val, 0, keepdims=True)
    return inv * (grad - first - unit_val * second)


def tile3(x):
    return jnp.concatenate([x, x, x], 1)


def column(row):
    return jnp.broadcast_to(row, (C, C)).T


def swap(x):
    return pltpu.roll(x, 64, 1)


def low_lanes(shape):
    return lax.broadcasted_iota(jnp.int32, shape, 1) < 64


def spread(src, dst):
    def body(i, _):
        at = pl.multiple_of(i * 8, 8)
        dst[pl.ds(pl.multiple_of(i * 192, 8), 192), :] = src[pl.ds(at, 8)].astype(F32).reshape(192, C)
        return 0

    lax.fori_loop(0, ROWS // 8, body, 0, unroll=2)


def gather_cols(src, q):
    base = C * COLS
    parts = [
        src[pl.ds(q, C, stride=COLS), :],
        src[pl.ds(q + HALF_COLS, C, stride=COLS), :],
        src[pl.ds(base + q, 64, stride=COLS), :],
        src[pl.ds(base + q + HALF_COLS, 64, stride=COLS), :],
    ]
    return jnp.concatenate(parts, 0).T


def row_code(mask_ref, chain_ref):
    half = lax.axis_index("half")
    code = jnp.where(mask_ref[...] > 0, chain_ref[...], -1)
    code = jnp.broadcast_to(code.reshape(1, RES), (8, RES))
    code = pltpu.roll(code, lax.rem(RES - half * ROWS, RES), 1)[:1]
    low = code[:, C : C + C]
    return code[:, :C], jnp.where(low_lanes((1, C)), low, swap(low))


def keep_row(q, codes, mask_s, chain_s, pairs_s):
    first = lax.axis_index("ch") * COLS + q
    factors = []
    for k in (first, first + HALF_COLS):
        chain = chain_s[k]
        factors.append([(pairs_s[c, chain] * mask_s[k]).astype(F32) for c in range(4)])

    def pick(code, factor):
        out = jnp.zeros(code.shape, F32)
        for c in range(4):
            out = jnp.where(code == c, factor[c], out)
        return out

    code_a, code_b = codes
    tail = jnp.where(low_lanes((1, C)), pick(code_b, factors[0]), pick(code_b, factors[1]))
    return jnp.concatenate([pick(code_a, factors[0]), pick(code_a, factors[1]), tail], 1)


def prepare(w_ref, wo_ref, gains, wt, wot, cols):
    wt[...] = w_ref[...].astype(F32).T.astype(BF16)
    wot[...] = wo_ref[...].astype(F32).T.astype(BF16)
    for n, g in enumerate(gains):
        cols[n] = column(g[...])


def front_kernel(
    pair_ref, tri_ref, cot_ref, mask_v, chain_v, mask_s, chain_s, pairs_s,
    w_ref, wo_ref, in_gain, in_bias, out_gain, out_bias, out_ref,
    xp, xt, xc, wt, wot, cols, stage,
):
    prepare(w_ref, wo_ref, (in_gain, in_bias, out_gain, out_bias), wt, wot, cols)
    spread(pair_ref, xp)
    spread(tri_ref, xt)
    spread(cot_ref, xc)
    codes = row_code(mask_v, chain_v)

    def put(row, value):
        stage[pl.ds(row, C, stride=OUT_ROWS), :] = value

    for r in range(4):
        put(36 + r, jnp.zeros((C, C), F32))

    def body(q, _):
        keep = keep_row(q, codes, mask_s, chain_s, pairs_s)
        z, _ = unit(gather_cols(xp, q))
        nz = (z * tile3(cols[0]) + tile3(cols[1])).astype(BF16)
        proj = dot(wt[...], nz)
        left = keep * sigmoid(proj[C : 2 * C]) * proj[:C]
        right = keep * sigmoid(proj[3 * C : 4 * C]) * proj[2 * C : 3 * C]
        outer = (gather_cols(xc, q) * sigmoid(proj[4 * C :])).astype(BF16)
        u, inv = unit(gather_cols(xt, q))
        grad = norm_back(dot(wo_ref[...], outer) * tile3(cols[2]), u, inv)
        put(G_A + q, grad[:, :C])
        put(G_A + HALF_COLS + q, grad[:, C : 2 * C])
        put(G_B + q, grad[:, 2 * C :])
        put(L_A + q, left[:, :C])
        put(L_A + HALF_COLS + q, left[:, C : 2 * C])
        put(R_A + q, right[:, :C])
        put(R_A + HALF_COLS + q, right[:, C : 2 * C])
        low = low_lanes((C, C))
        tail_l, tail_r = left[:, 2 * C :], right[:, 2 * C :]
        put(LR_B + q, jnp.where(low, tail_l, swap(tail_r)))
        put(LR_B + HALF_COLS + q, jnp.where(low, swap(tail_l), tail_r))
        return 0

    lax.fori_loop(0, HALF_COLS, body, 0, unroll=3)

    def flush(c, _):
        at = pl.multiple_of(c * OUT_ROWS, 8)
        out_ref[c] = stage[pl.ds(at, OUT_ROWS), :].astype(BF16)
        return 0

    lax.fori_loop(0, C, flush, 0, unroll=4)


def save_kernel(
    pair_ref, tri_ref, cot_ref, mask_v, chain_v, mask_s, chain_s, pairs_s,
    w_ref, wo_ref, in_gain, in_bias, out_gain, out_bias, saved_ref, inv_ref,
    xp, xt, xc, wt, wot, cols,
):
    prepare(w_ref, wo_ref, (in_gain, in_bias, out_gain, out_bias), wt, wot, cols)
    spread(pair_ref, xp)
    spread(tri_ref, xt)
    spread(cot_ref, xc)
    codes = row_code(mask_v, chain_v)

    def body(q, _):
        keep = keep_row(q, codes, mask_s, chain_s, pairs_s)
        z, inv_z = unit(gather_cols(xp, q))
        nz = (z * tile3(cols[0]) + tile3(cols[1])).astype(BF16)
        proj = dot(wt[...], nz)
        gate_l = sigmoid(proj[C : 2 * C])
        gate_r = sigmoid(proj[3 * C : 4 * C])
        gate_o = sigmoid(proj[4 * C :])
        u, _ = unit(gather_cols(xt, q))
        nx = (u * tile3(cols[2]) + tile3(cols[3])).astype(BF16)
        out_proj = dot(wot[...], nx)
        keep_l, keep_r = keep * gate_l, keep * gate_r
        saved_ref[q, 0] = keep_l.astype(BF16)
        saved_ref[q, 1] = (keep_l * proj[:C] * (1.0 - gate_l)).astype(BF16)
        saved_ref[q, 2] = keep_r.astype(BF16)
        saved_ref[q, 3] = (keep_r * proj[2 * C : 3 * C] * (1.0 - gate_r)).astype(BF16)
        saved_ref[q, 4] = (gather_cols(xc, q) * out_proj * gate_o * (1.0 - gate_o)).astype(BF16)
        saved_ref[q, 5] = z.astype(BF16)
        inv_ref[q] = jnp.broadcast_to(inv_z, (8, 3 * C))
        return 0

    lax.fori_loop(0, HALF_COLS, body, 0, unroll=3)


def channel_kernel(in_ref, out_ref, g, left, right, back_l, back_r):
    low24 = low_lanes((COLS, C))
    low12 = low_lanes((HALF_COLS, C))

    def take(w):
        blocks = [in_ref[w * 4 + h].astype(F32) for h in range(4)]
        rows_g = [b[G_A : G_A + COLS] for b in blocks]
        rows_l = [b[L_A : L_A + COLS] for b in blocks]
        rows_r = [b[R_A : R_A + COLS] for b in blocks]
        for h in (0, 2):
            a, b = blocks[h][G_B : G_B + HALF_COLS], blocks[h + 1][G_B : G_B + HALF_COLS]
            rows_g.append(jnp.concatenate([jnp.where(low12, a, swap(b)), jnp.where(low12, swap(a), b)], 0))
            a, b = blocks[h][LR_B : LR_B + COLS], blocks[h + 1][LR_B : LR_B + COLS]
            rows_l.append(jnp.where(low24, a, swap(b)))
            rows_r.append(jnp.where(low24, swap(a), b))
        return [jnp.concatenate(rows, 1) for rows in (rows_g, rows_l, rows_r)]

    def gather(pair, _):
        one, two = take(2 * pair), take(2 * pair + 1)
        at = pl.ds(pl.multiple_of(pair * 48, 16), 48)
        for ref, a, b in zip((g, left, right), one, two):
            ref[at, :] = jnp.concatenate([a, b], 0).astype(BF16)
        return 0

    lax.fori_loop(0, 16, gather, 0,unroll=2)
    spans = [(ROWS * h, C) for h in range(4)] + [(ROWS * h + C, 64) for h in range(4)]
    ordered = jnp.concatenate([g[at : at + size, :] for at, size in spans], 0)
    back_l[...] = dot(right[...], ordered)
    back_r[...] = lax.dot_general(left[...], ordered, (((1,), (1,)), ((), ())), preferred_element_type=F32)

    def give(w, _):
        at = pl.ds(pl.multiple_of(w * COLS, 8), COLS)
        for h in range(4):
            lanes = slice(h * C, (h + 1) * C)
            tail = slice((4 + h // 2) * C, (5 + h // 2) * C)
            a, b = back_l[at, tail], back_r[at, tail]
            mixed = jnp.where(low24, a, swap(b)) if h % 2 == 0 else jnp.where(low24, swap(a), b)
            out_ref[w * 4 + h] = jnp.concatenate([back_l[at, lanes], back_r[at, lanes], mixed], 0).astype(BF16)
        return 0

    lax.fori_loop(0, 32, give, 0, unroll=2)


def back_kernel(in_ref, saved_ref, inv_ref, w_ref, in_gain, out_ref, rows, cols, stage):
    cols[...] = column(in_gain[...])

    def fill(c, _):
        at = pl.multiple_of(c * BACK_ROWS, 8)
        rows[pl.ds(at, BACK_ROWS), :] = in_ref[c].astype(F32)
        return 0

    lax.fori_loop(0, C, fill, 0,unroll=4)

    def body(q, _):
        low = low_lanes((C, C))

        def get(row):
            return rows[pl.ds(row, C, stride=BACK_ROWS), :]

        a, b = get(48 + q), get(48 + HALF_COLS + q)
        tail_l = jnp.where(low, a, swap(b))
        tail_r = jnp.where(low, swap(a), b)
        grad_l = jnp.concatenate([get(q), get(HALF_COLS + q), tail_l], 1)
        grad_r = jnp.concatenate([get(COLS + q), get(COLS + HALF_COLS + q), tail_r], 1)
        grad_proj = jnp.concatenate(
            [
                (grad_l * saved_ref[q, 0].astype(F32)).astype(BF16),
                (grad_l * saved_ref[q, 1].astype(F32)).astype(BF16),
                (grad_r * saved_ref[q, 2].astype(F32)).astype(BF16),
                (grad_r * saved_ref[q, 3].astype(F32)).astype(BF16),
                saved_ref[q, 4],
            ],
            0,
        )
        e = dot(w_ref[...], grad_proj) * tile3(cols[...])
        grad = norm_back(e, saved_ref[q, 5].astype(F32), inv_ref[q][:1]).T
        base = C * COLS
        stage[pl.ds(q, C, stride=COLS), :] = grad[:C]
        stage[pl.ds(q + HALF_COLS, C, stride=COLS), :] = grad[C : 2 * C]
        stage[pl.ds(base + q, 64, stride=COLS), :] = grad[2 * C : 2 * C + 64]
        stage[pl.ds(base + q + HALF_COLS, 64, stride=COLS), :] = grad[2 * C + 64 :]
        return 0

    lax.fori_loop(0, HALF_COLS, body, 0, unroll=3)

    def flush(i, _):
        at = pl.multiple_of(i * 8, 8)
        rows8 = stage[pl.ds(pl.multiple_of(i * 192, 8), 192), :].reshape(8, COLS, C)
        out_ref[pl.ds(at, 8)] = rows8.astype(BF16)
        return 0

    lax.fori_loop(0, ROWS // 8, flush, 0)


def call(kernel, outs, scratch, args, smem=(), flops=0, moved=0, limit=69206016):
    scal = pl.BlockSpec(memory_space=pltpu.SMEM)

    def whole(x):
        return pl.BlockSpec(x.shape, lambda i: (0,) * len(x.shape))

    return pl.pallas_call(
        kernel,
        out_shape=outs,
        grid=(1,),
        in_specs=[scal if n in smem else whole(x) for n, x in enumerate(args)],
        out_specs=jax.tree.map(whole, outs),
        scratch_shapes=scratch,
        compiler_params=pltpu.CompilerParams(vmem_limit_bytes=limit),
        cost_estimate=pl.CostEstimate(flops=flops, bytes_accessed=moved, transcendentals=0),
    )(*args)


def exchange(x):
    return lax.all_to_all(x, AXES, split_axis=0, concat_axis=0, tiled=True)


def on_device(
    pair_act,
    tri_out,
    cotangent,
    residue_mask,
    chain_index,
    chain_pairs,
    in_weight,
    out_weight,
    in_gain,
    in_bias,
    out_gain,
    out_bias,
):
    shape = jax.ShapeDtypeStruct
    gains = [g.reshape(1, C) for g in (in_gain, in_bias, out_gain, out_bias)]
    given = [
        pair_act, tri_out, cotangent, residue_mask, chain_index,
        residue_mask, chain_index, chain_pairs, in_weight, out_weight, *gains,
    ]
    smem = (5, 6, 7)
    tile = pltpu.VMEM((ROWS * COLS, C), F32)
    shared = [tile, tile, tile, pltpu.VMEM((5 * C, C), BF16), pltpu.VMEM((C, C), BF16), pltpu.VMEM((4, C, C), F32)]
    sent = call(
        front_kernel,
        shape((C, OUT_ROWS, C), BF16),
        shared + [pltpu.VMEM((C * OUT_ROWS, C), F32)],
        given,
        smem,
        flops=2 * 4608 * 128 * 768,
        moved=8 << 20,
    )
    saved, inv = call(
        save_kernel,
        (shape((HALF_COLS, 6, C, 3 * C), BF16), shape((HALF_COLS, 8, 3 * C), F32)),
        shared,
        given,
        smem,
        flops=2 * 4608 * 128 * 768,
        moved=12 << 20,
    )
    got = exchange(sent)
    square = pltpu.VMEM((RES, RES), BF16)
    wide = pltpu.VMEM((RES, RES), F32)
    back = call(
        channel_kernel,
        shape((C, BACK_ROWS, C), BF16),
        [square, square, square, wide, wide],
        [got],
        flops=4 * RES**3,
        moved=8 << 20,
    )
    returned = exchange(back)
    return call(
        back_kernel,
        shape((ROWS, COLS, C), BF16),
        [pltpu.VMEM((C * BACK_ROWS, C), F32), pltpu.VMEM((C, C), F32), tile],
        [returned, saved, inv, in_weight, gains[0]],
        flops=2 * 4608 * 128 * 640,
        moved=12 << 20,
    )


def solution(mesh):
    return jax.shard_map(
        on_device,
        mesh=mesh,
        in_specs=(P("half", "ch", None),) * 3 + (P(),) * 9,
        out_specs=P("half", "ch", None),
        check_vma=False,
    )
```

```python
import jax
import jax.numpy as jnp
from jax import lax
from jax.experimental import pallas as pl
from jax.experimental.pallas import tpu as pltpu
from jax.sharding import PartitionSpec as P

EPSILON = 1e-05
AXES = ("ch", "half")
F32 = jnp.float32
BF16 = jnp.bfloat16

ROWS, COLS, C, RES = 192, 24, 128, 768
GROUP, PAIRS, GROUPS = 8, 4, 3
STEP, TAIL_AT, TAIL, OUT_ROWS = 32, 96, 16, 112
BACK_STEP, BACK_ROWS = 24, 72
X_PITCH, OUT_PITCH, TAIL_PITCH, BACK_PITCH = 9, 33, 17, 25
SPAN = 8


def dot(a, b):
    return jnp.dot(a, b, preferred_element_type=F32)


def mean(x):
    return jnp.sum(x, 0, keepdims=True) * (1.0 / C)


def centre(x):
    centred = x - mean(x)
    return centred, lax.rsqrt(mean(centred * centred) + EPSILON)


def column(row):
    return jnp.broadcast_to(row, (C, C)).T


def swap(x):
    return pltpu.roll(x, 64, 1)


def low_lanes(shape):
    return lax.broadcasted_iota(jnp.int32, shape, 1) < 64


def spread(src, dst):
    def body(i, _):
        values = src[pl.ds(pl.multiple_of(i * 16, 16), 16)].astype(F32)
        for n in range(16):
            dst[pl.ds((i * 16 + n) * X_PITCH, GROUP), :] = values[n]
        return 0

    lax.fori_loop(0, ROWS // 16, body, 0, unroll=2)


def gather(src, q, part):
    if part < 2:
        return src[pl.ds(q + PAIRS * part, C, stride=X_PITCH), :].T
    base = C * X_PITCH
    tails = [src[pl.ds(base + q + PAIRS * n, 64, stride=X_PITCH), :] for n in range(2)]
    return jnp.concatenate(tails, 0).T


def row_code(mask_ref, chain_ref):
    half = lax.axis_index("half")
    code = jnp.where(mask_ref[...] > 0, chain_ref[...], -1)
    code = jnp.broadcast_to(code.reshape(1, RES), (8, RES))
    code = pltpu.roll(code, lax.rem(RES - half * ROWS, RES), 1)[:1]
    tail = code[:, C : C + C]
    return code[:, :C], jnp.where(low_lanes((1, C)), tail, swap(tail))


def keep_rows(q, codes, mask_s, chain_s, pairs_s):
    first = lax.axis_index("ch") * COLS + q

    def pick(code, k):
        chain, out = chain_s[k], jnp.zeros(code.shape, F32)
        for c in range(4):
            out = jnp.where(code == c, 0.5 * (pairs_s[c, chain] * mask_s[k]).astype(F32), out)
        return out

    code_a, code_b = codes
    tail = jnp.where(low_lanes((1, C)), pick(code_b, first), pick(code_b, first + PAIRS))
    return pick(code_a, first), pick(code_a, first + PAIRS), tail


def prepare(w_ref, wo_ref, gains, wt, wot, cols):
    for n in range(5):
        part = w_ref[:, n * C : (n + 1) * C].astype(F32).T
        wt[n] = (part * 0.5 if n in (1, 3, 4) else part).astype(BF16)
    wot[...] = wo_ref[...].astype(F32).T.astype(BF16)
    for n, g in enumerate(gains):
        cols[n] = column(g[...])
    cols[4] = cols[2] * 0.5


def front_kernel(
    pair_ref, tri_ref, cot_ref, mask_v, chain_v, mask_s, chain_s, pairs_s,
    w_ref, wo_ref, in_gain, in_bias, out_gain, out_bias, out_ref,
    xp, xt, xc, wt, wot, cols, stage, stage_tail, packed, sems,
):
    group = pl.program_id(0)

    @pl.when(group == 0)
    def _():
        prepare(w_ref, wo_ref, (in_gain, in_bias, out_gain, out_bias), wt, wot, cols)
        for r in range(4):
            stage_tail[pl.ds(12 + r, C, stride=TAIL_PITCH), :] = jnp.zeros((C, C), F32)

    spread(pair_ref, xp)
    spread(tri_ref, xt)
    spread(cot_ref, xc)
    codes = row_code(mask_v, chain_v)

    def put(row, value):
        stage[pl.ds(row, C, stride=OUT_PITCH), :] = value

    def body(q, _):
        keeps = keep_rows(group * GROUP + q, codes, mask_s, chain_s, pairs_s)
        for part in range(3):
            centred, inv = centre(gather(xp, q, part))
            nz = (centred * inv * cols[0] + cols[1]).astype(BF16)
            keep = keeps[part]
            left = (jnp.tanh(dot(wt[1], nz)) + 1.0) * (dot(wt[0], nz) * keep)
            right = (jnp.tanh(dot(wt[3], nz)) + 1.0) * (dot(wt[2], nz) * keep)
            outer = ((jnp.tanh(dot(wt[4], nz)) + 1.0) * gather(xc, q, part)).astype(BF16)
            centred, inv = centre(gather(xt, q, part))
            h = dot(wo_ref[...], outer) * cols[4]
            second = mean(h * centred) * (inv * inv)
            grad = inv * (h - mean(h) - centred * second)
            if part < 2:
                put(q + PAIRS * part, grad)
                put(GROUP + q + PAIRS * part, left)
                put(2 * GROUP + q + PAIRS * part, right)
            else:
                low = low_lanes((C, C))
                stage_tail[pl.ds(group * PAIRS + q, C, stride=TAIL_PITCH), :] = grad
                put(3 * GROUP + q, jnp.where(low, left, swap(right)))
                put(3 * GROUP + PAIRS + q, jnp.where(low, swap(left), right))
        return 0

    lax.fori_loop(0, PAIRS, body, 0, unroll=4)

    def send(n):
        rows = pl.ds(n * STEP, STEP)
        return pltpu.make_async_copy(packed.at[:, rows], out_ref.at[:, rows], sems.at[n])

    tail = pl.ds(TAIL_AT, TAIL)
    send_tail = pltpu.make_async_copy(packed.at[:, tail], out_ref.at[:, tail], sems.at[GROUPS])
    for n in range(GROUPS):

        @pl.when(group == n)
        def _(n=n):
            def flush(c, _):
                packed[c, n * STEP : (n + 1) * STEP] = stage[pl.ds(c * OUT_PITCH, STEP), :].astype(BF16)
                return 0

            lax.fori_loop(0, C, flush, 0, unroll=8)
            send(n).start()

    @pl.when(group == GROUPS - 1)
    def _():
        def flush(c, _):
            packed[c, TAIL_AT:] = stage_tail[pl.ds(c * TAIL_PITCH, TAIL), :].astype(BF16)
            return 0

        lax.fori_loop(0, C, flush, 0, unroll=8)
        send_tail.start()
        for n in range(GROUPS):
            send(n).wait()
        send_tail.wait()


def save_kernel(
    pair_ref, tri_ref, cot_ref, mask_v, chain_v, mask_s, chain_s, pairs_s,
    w_ref, wo_ref, in_gain, in_bias, out_gain, out_bias, saved_ref, inv_ref,
    xp, xt, xc, wt, wot, cols,
):
    group = pl.program_id(0)

    @pl.when(group == 0)
    def _():
        prepare(w_ref, wo_ref, (in_gain, in_bias, out_gain, out_bias), wt, wot, cols)

    spread(pair_ref, xp)
    spread(tri_ref, xt)
    spread(cot_ref, xc)
    codes = row_code(mask_v, chain_v)

    def body(q, _):
        keeps = keep_rows(group * GROUP + q, codes, mask_s, chain_s, pairs_s)
        for part in range(3):
            centred, inv = centre(gather(xp, q, part))
            unit_z = centred * inv
            nz = (unit_z * cols[0] + cols[1]).astype(BF16)
            keep = keeps[part]
            for n in (0, 1):
                gate = jnp.tanh(dot(wt[2 * n + 1], nz))
                kept = (gate + 1.0) * keep
                saved_ref[q, part, 2 * n] = kept.astype(BF16)
                saved_ref[q, part, 2 * n + 1] = (kept * dot(wt[2 * n], nz) * (0.5 - 0.5 * gate)).astype(BF16)
            gate = jnp.tanh(dot(wt[4], nz))
            centred, inv_x = centre(gather(xt, q, part))
            nx = (centred * inv_x * cols[2] + cols[3]).astype(BF16)
            slope = (0.5 + 0.5 * gate) * (0.5 - 0.5 * gate)
            saved_ref[q, part, 4] = (gather(xc, q, part) * dot(wot[...], nx) * slope).astype(BF16)
            saved_ref[q, part, 5] = unit_z.astype(BF16)
            inv_ref[q, part] = jnp.broadcast_to(inv, (8, C))
        return 0

    lax.fori_loop(0, PAIRS, body, 0)


def channel_kernel(in_ref, out_ref, g, left, right, ordered):
    step = pl.program_id(0)
    steps = 32 // SPAN
    low8, low16 = low_lanes((GROUP, C)), low_lanes((TAIL, C))

    def take(w):
        blocks = [in_ref[w * 4 + h].astype(F32) for h in range(4)]

        def part(n):
            return [jnp.concatenate([b[STEP * m + GROUP * n : STEP * m + GROUP * (n + 1)] for m in range(3)], 0) for b in blocks]

        rows_g, rows_l, rows_r, mixed = part(0), part(1), part(2), part(3)
        low24 = low_lanes((COLS, C))
        for h in (0, 2):
            a, b = blocks[h][TAIL_AT:], blocks[h + 1][TAIL_AT:]
            one, two = jnp.where(low16, a, swap(b)), jnp.where(low16, swap(a), b)
            pieces = [x[PAIRS * m : PAIRS * (m + 1)] for m in range(3) for x in (one, two)]
            rows_g.append(jnp.concatenate(pieces, 0))
            a, b = mixed[h], mixed[h + 1]
            rows_l.append(jnp.where(low24, a, swap(b)))
            rows_r.append(jnp.where(low24, swap(a), b))
        return [jnp.concatenate(rows, 1) for rows in (rows_g, rows_l, rows_r)]

    @pl.when(step < steps)
    def _():
        def body(pair, _):
            one, two = take(2 * pair), take(2 * pair + 1)
            at = pl.ds(pl.multiple_of(step * (SPAN * COLS) + pair * 48, 16), 48)
            for ref, a, b in zip((g, left, right), one, two):
                ref[at, :] = jnp.concatenate([a, b], 0).astype(BF16)
            return 0

        lax.fori_loop(0, SPAN // 2, body, 0, unroll=2)

    @pl.when(step == steps)
    def _():
        to = 0
        for at, size in [(ROWS * h, C) for h in range(4)] + [(ROWS * h + C, 64) for h in range(4)]:
            ordered[to : to + size] = g[at : at + size]
            to += size

    @pl.when(step >= steps)
    def _():
        rows = pl.ds(pl.multiple_of((step - steps) * (SPAN * COLS), SPAN * COLS), SPAN * COLS)
        back_l = dot(right[rows, :], ordered[...])
        back_r = lax.dot_general(left[rows, :], ordered[...], (((1,), (1,)), ((), ())), preferred_element_type=F32)
        for w in range(SPAN):
            for h in range(4):
                lanes, tail = slice(h * C, (h + 1) * C), slice((4 + h // 2) * C, (5 + h // 2) * C)
                pieces = []
                for m in range(3):
                    at = slice(w * COLS + m * GROUP, w * COLS + (m + 1) * GROUP)
                    a, b = back_l[at, tail], back_r[at, tail]
                    mixed = jnp.where(low8, a, swap(b)) if h % 2 == 0 else jnp.where(low8, swap(a), b)
                    pieces += [back_l[at, lanes], back_r[at, lanes], mixed]
                out_ref[w * 4 + h] = jnp.concatenate(pieces, 0).astype(BF16)


def back_kernel(in_ref, saved_ref, inv_ref, w_ref, in_gain, out_ref, rows, cols, stage):
    group = pl.program_id(0)

    @pl.when(group == 0)
    def _():
        cols[...] = column(in_gain[...])

    def fill(c, _):
        rows[pl.ds(c * BACK_PITCH, BACK_STEP), :] = in_ref[c].astype(F32)
        return 0

    lax.fori_loop(0, C, fill, 0, unroll=8)

    def body(q, _):
        low = low_lanes((C, C))

        def get(row):
            return rows[pl.ds(row, C, stride=BACK_PITCH), :]

        a, b = get(2 * GROUP + q), get(2 * GROUP + PAIRS + q)
        lefts = [get(q), get(PAIRS + q), jnp.where(low, a, swap(b))]
        rights = [get(GROUP + q), get(GROUP + PAIRS + q), jnp.where(low, swap(a), b)]
        for part in range(3):
            saved = saved_ref.at[q, part]
            grad_l, grad_r = lefts[part].astype(BF16), rights[part].astype(BF16)
            pieces = [grad_l * saved[0], grad_l * saved[1], grad_r * saved[2], grad_r * saved[3], saved[4]]
            e = dot(w_ref[...], jnp.concatenate(pieces, 0)) * cols[...]
            unit_z = saved[5].astype(F32)
            grad = (inv_ref[q, part][:1] * (e - mean(e) - unit_z * mean(e * unit_z))).T
            if part < 2:
                stage[pl.ds(q + PAIRS * part, C, stride=X_PITCH), :] = grad
            else:
                base = C * X_PITCH
                stage[pl.ds(base + q, 64, stride=X_PITCH), :] = grad[:64]
                stage[pl.ds(base + q + PAIRS, 64, stride=X_PITCH), :] = grad[64:]
        return 0

    lax.fori_loop(0, PAIRS, body, 0, unroll=4)

    def flush(i, _):
        at = pl.multiple_of(i * 16, 16)
        rows16 = [stage[pl.ds((i * 16 + n) * X_PITCH, GROUP), :].reshape(1, GROUP, C) for n in range(16)]
        out_ref[pl.ds(at, 16)] = jnp.concatenate(rows16, 0).astype(BF16)
        return 0

    lax.fori_loop(0, ROWS // 16, flush, 0, unroll=2)


def whole(x):
    return pl.BlockSpec(x.shape, lambda i: (0,) * len(x.shape))


def call(kernel, grid, ins, outs, out_specs, scratch, args, flops, moved):
    return pl.pallas_call(
        kernel,
        out_shape=outs,
        grid=(grid,),
        in_specs=ins,
        out_specs=out_specs,
        scratch_shapes=scratch,
        compiler_params=pltpu.CompilerParams(vmem_limit_bytes=66 << 20),
        cost_estimate=pl.CostEstimate(flops=flops, bytes_accessed=moved, transcendentals=0),
    )(*args)


def exchange(x):
    return lax.all_to_all(x, AXES, split_axis=0, concat_axis=0, tiled=True)


def on_device(
    pair_act,
    tri_out,
    cotangent,
    residue_mask,
    chain_index,
    chain_pairs,
    in_weight,
    out_weight,
    in_gain,
    in_bias,
    out_gain,
    out_bias,
):
    shape = jax.ShapeDtypeStruct
    gains = [g.reshape(1, C) for g in (in_gain, in_bias, out_gain, out_bias)]
    given = [
        pair_act, tri_out, cotangent, residue_mask, chain_index,
        residue_mask, chain_index, chain_pairs, in_weight, out_weight, *gains,
    ]
    scalars = pl.BlockSpec(memory_space=pltpu.SMEM)
    tile = pl.BlockSpec((ROWS, GROUP, C), lambda i: (0, i, 0))
    given_specs = [tile] * 3 + [whole(x) for x in given[3:5]] + [scalars] * 3 + [whole(x) for x in given[8:]]
    part = pltpu.VMEM((ROWS * X_PITCH, C), F32)
    shared = [part, part, part, pltpu.VMEM((5, C, C), BF16), pltpu.VMEM((C, C), BF16), pltpu.VMEM((5, C, C), F32)]
    sent = call(
        front_kernel,
        GROUPS,
        given_specs,
        shape((C, OUT_ROWS, C), BF16),
        pl.BlockSpec(memory_space=pl.ANY),
        shared
        + [
            pltpu.VMEM((C * OUT_PITCH, C), F32),
            pltpu.VMEM((C * TAIL_PITCH, C), F32),
            pltpu.VMEM((C, OUT_ROWS, C), BF16),
            pltpu.SemaphoreType.DMA((GROUPS + 1,)),
        ],
        given,
        2 * 4608 * 128 * 768,
        8 << 20,
    )
    saved, inv = call(
        save_kernel,
        GROUPS,
        given_specs,
        (shape((GROUPS * PAIRS, 3, 6, C, C), BF16), shape((GROUPS * PAIRS, 3, 8, C), F32)),
        (
            pl.BlockSpec((PAIRS, 3, 6, C, C), lambda i: (i, 0, 0, 0, 0)),
            pl.BlockSpec((PAIRS, 3, 8, C), lambda i: (i, 0, 0, 0)),
        ),
        shared,
        given,
        2 * 4608 * 128 * 768,
        12 << 20,
    )
    got = exchange(sent)
    square = pltpu.VMEM((RES, RES), BF16)
    steps = 32 // SPAN
    back = call(
        channel_kernel,
        2 * steps,
        [pl.BlockSpec((4 * SPAN, OUT_ROWS, C), lambda i: (jnp.minimum(i, steps - 1), 0, 0))],
        shape((C, BACK_ROWS, C), BF16),
        pl.BlockSpec((4 * SPAN, BACK_ROWS, C), lambda i: (jnp.maximum(i - steps, 0), 0, 0)),
        [square, square, square, square],
        [got],
        4 * RES**3,
        8 << 20,
    )
    returned = exchange(back)
    return call(
        back_kernel,
        GROUPS,
        [
            pl.BlockSpec((C, BACK_STEP, C), lambda i: (0, i, 0)),
            pl.BlockSpec((PAIRS, 3, 6, C, C), lambda i: (i, 0, 0, 0, 0)),
            pl.BlockSpec((PAIRS, 3, 8, C), lambda i: (i, 0, 0, 0)),
            whole(in_weight),
            whole(gains[0]),
        ],
        shape((ROWS, COLS, C), BF16),
        tile,
        [pltpu.VMEM((C * BACK_PITCH, C), F32), pltpu.VMEM((C, C), F32), part],
        [returned, saved, inv, in_weight, gains[0]],
        2 * 4608 * 128 * 640,
        12 << 20,
    )


def solution(mesh):
    return jax.shard_map(
        on_device,
        mesh=mesh,
        in_specs=(P("half", "ch", None),) * 3 + (P(),) * 9,
        out_specs=P("half", "ch", None),
        check_vma=False,
    )
```

```python
import jax
import jax.numpy as jnp
from jax import lax
from jax.experimental import pallas as pl
from jax.experimental.pallas import tpu as pltpu
from jax.sharding import PartitionSpec as P

EPSILON = 1e-05
AXES = ("ch", "half")
F32 = jnp.float32
BF16 = jnp.bfloat16

ROWS, COLS, C, RES = 192, 24, 128, 768
GROUP, PAIRS, GROUPS = 8, 4, 3
STEP, TAIL_AT, TAIL, OUT_ROWS = 32, 96, 16, 112
BACK_STEP, BACK_ROWS = 24, 72
X_PITCH, OUT_PITCH, TAIL_PITCH, BACK_PITCH = GROUP + 1, STEP + 1, TAIL + 1, BACK_STEP + 1
X_SIZE, OUT_SIZE, BACK_SIZE = ROWS * X_PITCH, C * OUT_PITCH, C * BACK_PITCH
FETCHES = 8
CHUNKS = 4
CHUNK = RES // CHUNKS


def dot(a, b):
    return jnp.dot(a, b, preferred_element_type=F32)


def mean(x):
    return jnp.sum(x, 0, keepdims=True) * (1.0 / C)


def centre(x):
    centred = x - mean(x)
    return centred, lax.rsqrt(mean(centred * centred) + EPSILON)


def column(row):
    return jnp.broadcast_to(row[...].reshape(1, C), (C, C)).T


def swap(x):
    return pltpu.roll(x, 64, 1)


def low_lanes(shape):
    return lax.broadcasted_iota(jnp.int32, shape, 1) < 64


def copies(sources, targets, sems):
    started = [pltpu.make_async_copy(s, t, sems.at[n]) for n, (s, t) in enumerate(zip(sources, targets))]
    for copy in started:
        copy.start()
    return started


def spread(tiles, x, group):
    for n in range(3):

        def body(i, _):
            values = tiles[group, n, pl.ds(pl.multiple_of(i * 16, 16), 16)].astype(F32)
            for m in range(16):
                x[n, pl.ds((i * 16 + m) * X_PITCH, GROUP), :] = values[m]
            return 0

        lax.fori_loop(0, ROWS // 16, body, 0, unroll=2)


def gather(x, n, q, part):
    if part < 2:
        return x[n, pl.ds(q + PAIRS * part, C, stride=X_PITCH), :].T
    base = C * X_PITCH + q
    return jnp.concatenate([x[n, pl.ds(base + PAIRS * m, 64, stride=X_PITCH), :] for m in range(2)], 0).T


def find_keep(mask_v, chain_v, pairs_v, keep):
    code = jnp.where(mask_v[...] > 0, chain_v[...], -1)
    code = jnp.broadcast_to(code.reshape(1, RES), (8, RES))
    rows = pltpu.roll(code, lax.rem(RES - lax.axis_index("half") * ROWS, RES), 1)[:1]
    cols = pltpu.roll(code, lax.rem(RES - lax.axis_index("ch") * COLS, RES), 1)[:1, :C]
    cols = jnp.broadcast_to(cols, (C, C)).astype(F32).T[:COLS]
    tail = rows[:, C : 2 * C]
    tail = jnp.where(low_lanes((1, C)), tail, swap(tail))
    pairs = pairs_v[...].astype(F32) * 0.5
    for n, rows_n in enumerate((rows[:, :C], tail)):
        out = jnp.zeros((COLS, C), F32)
        for d in range(4):
            across = jnp.zeros((1, C), F32)
            for c in range(4):
                across = jnp.where(rows_n == c, jnp.broadcast_to(pairs[c : c + 1, d : d + 1], (1, C)), across)
            out = jnp.where(cols == float(d), jnp.broadcast_to(across, (COLS, C)), out)
        keep[n] = out


def keep_of(keep, col, part):
    if part < 2:
        return keep[0, pl.ds(col + PAIRS * part, 1), :]
    return jnp.where(low_lanes((1, C)), keep[1, pl.ds(col, 1), :], keep[1, pl.ds(col + PAIRS, 1), :])


def prepare(given, buffers, wt, wot, cols, keep, sems):
    mask_v, chain_v, pairs_v, w_v, wo_v, *gains, tiles = buffers
    started = copies(given[3:], buffers[:-1], sems)

    def tile(group, n):
        at = pl.ds(pl.multiple_of(group * GROUP, GROUP), GROUP)
        return pltpu.make_async_copy(given[n].at[:, at], tiles.at[group, n], sems.at[9 + group * 3 + n])

    for group in range(GROUPS):
        for n in range(3):
            tile(group, n).start()
    for copy in started:
        copy.wait()
    for n in range(5):
        part = w_v[:, n * C : (n + 1) * C].astype(F32).T
        wt[n] = (part * 0.5 if n in (1, 3, 4) else part).astype(BF16)
    wot[...] = wo_v[...].astype(F32).T.astype(BF16)
    for n, g in enumerate(gains):
        cols[n] = column(g)
    cols[4] = cols[2] * 0.5
    find_keep(mask_v, chain_v, pairs_v, keep)

    def wait(group):
        for n in range(3):
            tile(group, n).wait()

    return wait


def front_kernel(*refs):
    given, out_ref = refs[:12], refs[12]
    *buffers, x, wt, wot, cols, keep, stage, stage_tail, packed, sems, out_sems = refs[13:]
    wo_v, tiles = buffers[4], buffers[-1]
    wait = prepare(given, buffers, wt, wot, cols, keep, sems)
    for r in range(4):
        stage_tail[pl.ds(12 + r, C, stride=TAIL_PITCH), :] = jnp.zeros((C, C), F32)

    def send(group):
        rows = pl.ds(pl.multiple_of(group * STEP, STEP), STEP)
        return pltpu.make_async_copy(packed.at[:, rows], out_ref.at[:, rows], out_sems.at[group])

    def body(group, _):
        wait(group)
        spread(tiles, x, group)
        for q in range(PAIRS):
            col = group * GROUP + q

            def put(row, value):
                stage[pl.ds(row, C, stride=OUT_PITCH), :] = value

            for part in range(3):
                centred, inv = centre(gather(x, 0, q, part))
                nz = (centred * inv * cols[0] + cols[1]).astype(BF16)
                kept = keep_of(keep, col, part)
                left = (jnp.tanh(dot(wt[1], nz)) + 1.0) * (dot(wt[0], nz) * kept)
                right = (jnp.tanh(dot(wt[3], nz)) + 1.0) * (dot(wt[2], nz) * kept)
                outer = ((jnp.tanh(dot(wt[4], nz)) + 1.0) * gather(x, 2, q, part)).astype(BF16)
                centred, inv = centre(gather(x, 1, q, part))
                h = dot(wo_v[...], outer) * cols[4]
                second = mean(h * centred) * (inv * inv)
                grad = inv * (h - mean(h) - centred * second)
                if part < 2:
                    put(q + PAIRS * part, grad)
                    put(GROUP + q + PAIRS * part, left)
                    put(2 * GROUP + q + PAIRS * part, right)
                else:
                    low = low_lanes((C, C))
                    stage_tail[pl.ds(group * PAIRS + q, C, stride=TAIL_PITCH), :] = grad
                    put(3 * GROUP + q, jnp.where(low, left, swap(right)))
                    put(3 * GROUP + PAIRS + q, jnp.where(low, swap(left), right))

        def pack(c, _):
            rows = pl.ds(pl.multiple_of(group * STEP, STEP), STEP)
            packed[c, rows] = stage[pl.ds(c * OUT_PITCH, STEP), :].astype(BF16)
            return 0

        lax.fori_loop(0, C, pack, 0, unroll=8)

        @pl.when(group < GROUPS - 1)
        def _():
            send(group).start()

        return 0

    lax.fori_loop(0, GROUPS, body, 0)

    def pack(c, _):
        packed[c, TAIL_AT:] = stage_tail[pl.ds(c * TAIL_PITCH, TAIL), :].astype(BF16)
        return 0

    lax.fori_loop(0, C, pack, 0, unroll=8)
    rest = pl.ds((GROUPS - 1) * STEP, OUT_ROWS - (GROUPS - 1) * STEP)
    final = pltpu.make_async_copy(packed.at[:, rest], out_ref.at[:, rest], out_sems.at[GROUPS - 1])
    final.start()
    for group in range(GROUPS - 1):
        send(group).wait()
    final.wait()


def save_kernel(*refs):
    given, saved_ref, inv_ref = refs[:12], refs[12], refs[13]
    *buffers, x, wt, wot, cols, keep, sems = refs[14:]
    tiles = buffers[-1]
    wait = prepare(given, buffers, wt, wot, cols, keep, sems)

    def body(group, _):
        wait(group)
        spread(tiles, x, group)

        def pair(q, _):
            n, col = group * PAIRS + q, group * GROUP + q
            for part in range(3):
                centred, inv = centre(gather(x, 0, q, part))
                unit_z = centred * inv
                nz = (unit_z * cols[0] + cols[1]).astype(BF16)
                kept_by = keep_of(keep, col, part)
                for m in (0, 1):
                    gate = jnp.tanh(dot(wt[2 * m + 1], nz))
                    kept = (gate + 1.0) * kept_by
                    saved_ref[n, part, 2 * m] = kept.astype(BF16)
                    saved_ref[n, part, 2 * m + 1] = (kept * dot(wt[2 * m], nz) * (0.5 - 0.5 * gate)).astype(BF16)
                gate = jnp.tanh(dot(wt[4], nz))
                centred, inv_x = centre(gather(x, 1, q, part))
                nx = (centred * inv_x * cols[2] + cols[3]).astype(BF16)
                slope = (0.5 + 0.5 * gate) * (0.5 - 0.5 * gate)
                saved_ref[n, part, 4] = (gather(x, 2, q, part) * dot(wot[...], nx) * slope).astype(BF16)
                saved_ref[n, part, 5] = unit_z.astype(BF16)
                inv_ref[n, part] = jnp.broadcast_to(inv, (8, C))
            return 0

        lax.fori_loop(0, PAIRS, pair, 0)
        return 0

    lax.fori_loop(0, GROUPS, body, 0)


def channel_kernel(in_v, out_ref, g, left, right, out_v, sems):
    low8, low16, low24 = (low_lanes((n, C)) for n in (GROUP, TAIL, COLS))

    def take(w):
        blocks = [in_v[w * 4 + h].astype(F32) for h in range(4)]

        def part(n):
            at = [STEP * m + GROUP * n for m in range(3)]
            return [jnp.concatenate([b[a : a + GROUP] for a in at], 0) for b in blocks]

        rows_g, rows_l, rows_r, mixed = part(0), part(1), part(2), part(3)
        for h in (0, 2):
            a, b = blocks[h][TAIL_AT:], blocks[h + 1][TAIL_AT:]
            one, two = jnp.where(low16, a, swap(b)), jnp.where(low16, swap(a), b)
            pieces = [v[PAIRS * m : PAIRS * (m + 1)] for m in range(3) for v in (one, two)]
            rows_g.append(jnp.concatenate(pieces, 0))
            a, b = mixed[h], mixed[h + 1]
            rows_l.append(jnp.where(low24, a, swap(b)))
            rows_r.append(jnp.where(low24, swap(a), b))
        return [jnp.concatenate(rows, 1) for rows in (rows_g, rows_l, rows_r)]

    def move(pair):
        one, two = take(2 * pair), take(2 * pair + 1)
        at = pl.ds(pl.multiple_of(pair * 48, 16), 48)
        both = [jnp.concatenate([a, b], 0).astype(BF16) for a, b in zip(one, two)]
        left[at, :] = both[1]
        right[at, :] = both[2]
        for n in range(3):
            block = pair * 3 + n
            half = block // 12
            rest = block - half * 12
            to = jnp.where(rest < 8, half * 8 + rest, 32 + half * 4 + rest - 8)
            g[pl.ds(pl.multiple_of(to * 16, 16), 16), :] = both[0][n * 16 : (n + 1) * 16]

    def body(n, _):
        for pair in range(16 // FETCHES):
            move(n * (16 // FETCHES) + pair)
        return 0

    lax.fori_loop(0, FETCHES, body, 0)

    def send(n):
        part = pl.ds(n * (C // CHUNKS), C // CHUNKS)
        return pltpu.make_async_copy(out_v.at[part], out_ref.at[part], sems.at[n])

    for n in range(CHUNKS):
        rows = slice(n * CHUNK, (n + 1) * CHUNK)
        back_l = dot(right[rows, :], g[...])
        back_r = lax.dot_general(left[rows, :], g[...], (((1,), (1,)), ((), ())), preferred_element_type=F32)
        for w in range(CHUNK // COLS):
            for h in range(4):
                lanes, tail = slice(h * C, (h + 1) * C), slice((4 + h // 2) * C, (5 + h // 2) * C)
                pieces = []
                for m in range(3):
                    at = slice(w * COLS + m * GROUP, w * COLS + (m + 1) * GROUP)
                    a, b = back_l[at, tail], back_r[at, tail]
                    mixed = jnp.where(low8, a, swap(b)) if h % 2 == 0 else jnp.where(low8, swap(a), b)
                    pieces += [back_l[at, lanes], back_r[at, lanes], mixed]
                out_v[(n * (CHUNK // COLS) + w) * 4 + h] = jnp.concatenate(pieces, 0).astype(BF16)
        send(n).start()
    for n in range(CHUNKS):
        send(n).wait()


def back_kernel(
    in_ref, saved_ref, inv_ref, w_ref, gain_ref, out_ref,
    in_v, saved_v, inv_v, w_v, gain_v, rows, cols, stage, out_v, in_sems, sems, out_sems,
):

    def fetch(n):
        at = pl.ds(pl.multiple_of(n * BACK_STEP, 8), BACK_STEP)
        return pltpu.make_async_copy(in_ref.at[:, at], in_v.at[n], in_sems.at[n])

    started = copies([w_ref, gain_ref, inv_ref], [w_v, gain_v, inv_v], sems)

    def take(group):
        at = pl.ds(group * PAIRS, PAIRS)
        return pltpu.make_async_copy(saved_ref.at[at], saved_v.at[at], sems.at[3 + group])

    for group in range(GROUPS):
        fetch(group).start()
        take(group).start()
    low = low_lanes((C, C))

    def send(group):
        at = pl.ds(pl.multiple_of(group * GROUP, GROUP), GROUP)
        return pltpu.make_async_copy(out_v.at[group], out_ref.at[:, at], out_sems.at[group])

    for copy in started:
        copy.wait()
    cols[...] = column(gain_v)

    def body(group, _):
        fetch(group).wait()

        def fill(c, _):
            rows[pl.ds(c * BACK_PITCH, BACK_STEP), :] = in_v[group, c].astype(F32)
            return 0

        lax.fori_loop(0, C, fill, 0, unroll=8)
        take(group).wait()

        def get(row):
            return rows[pl.ds(row, C, stride=BACK_PITCH), :]

        def put(row, value):
            stage[pl.ds(row, value.shape[0], stride=X_PITCH), :] = value

        for q in range(PAIRS):
            n = group * PAIRS + q
            a, b = get(2 * GROUP + q), get(2 * GROUP + PAIRS + q)
            lefts = [get(q), get(PAIRS + q), jnp.where(low, a, swap(b))]
            rights = [get(GROUP + q), get(GROUP + PAIRS + q), jnp.where(low, swap(a), b)]
            for part in range(3):
                saved = saved_v.at[n, part]
                grad_l, grad_r = lefts[part].astype(BF16), rights[part].astype(BF16)
                pieces = [grad_l * saved[0], grad_l * saved[1], grad_r * saved[2], grad_r * saved[3], saved[4]]
                e = dot(w_v[...], jnp.concatenate(pieces, 0)) * cols[...]
                unit_z = saved[5].astype(F32)
                grad = (inv_v[n, part][:1] * (e - mean(e) - unit_z * mean(e * unit_z))).T
                if part < 2:
                    put(q + PAIRS * part, grad)
                else:
                    put(C * X_PITCH + q, grad[:64])
                    put(C * X_PITCH + PAIRS + q, grad[64:])

        def flush(i, _):
            found = [stage[pl.ds((i * 16 + m) * X_PITCH, GROUP), :].reshape(1, GROUP, C) for m in range(16)]
            out_v[group, pl.ds(i * 16, 16)] = jnp.concatenate(found, 0).astype(BF16)
            return 0

        lax.fori_loop(0, ROWS // 16, flush, 0, unroll=2)
        send(group).start()
        return 0

    lax.fori_loop(0, GROUPS, body, 0)
    for group in range(GROUPS):
        send(group).wait()


HBM = pl.BlockSpec(memory_space=pltpu.HBM)
VMEM = pl.BlockSpec(memory_space=pltpu.VMEM)


def call(kernel, ins, outs, out_specs, scratch, args, limit, flops, moved):
    return pl.pallas_call(
        kernel,
        out_shape=outs,
        in_specs=ins,
        out_specs=out_specs,
        scratch_shapes=scratch,
        compiler_params=pltpu.CompilerParams(vmem_limit_bytes=limit << 20),
        cost_estimate=pl.CostEstimate(flops=flops, bytes_accessed=moved, transcendentals=0),
    )(*args)


def exchange(x):
    return lax.all_to_all(x, AXES, split_axis=0, concat_axis=0, tiled=True)


def on_device(*given):
    shape, vmem, dma = jax.ShapeDtypeStruct, pltpu.VMEM, pltpu.SemaphoreType.DMA
    in_weight, in_gain = given[6], given[8]
    buffers = [
        *(vmem(v.shape, v.dtype) for v in given[3:]),
        vmem((GROUPS, 3, ROWS, GROUP, C), BF16),
        vmem((3, X_SIZE, C), F32),
        vmem((5, C, C), BF16),
        vmem((C, C), BF16),
        vmem((5, C, C), F32),
        vmem((2, COLS, C), F32),
    ]
    sent = call(
        front_kernel,
        [HBM] * 12,
        shape((C, OUT_ROWS, C), BF16),
        HBM,
        [
            *buffers,
            vmem((OUT_SIZE, C), F32),
            vmem((C * TAIL_PITCH, C), F32),
            vmem((C, OUT_ROWS, C), BF16),
            dma((18,)),
            dma((GROUPS,)),
        ],
        given,
        66,
        2 * 4608 * 128 * 768,
        8 << 20,
    )
    saved, inv = call(
        save_kernel,
        [HBM] * 12,
        (shape((GROUPS * PAIRS, 3, 6, C, C), BF16), shape((GROUPS * PAIRS, 3, 8, C), F32)),
        (VMEM, VMEM),
        [*buffers, dma((18,))],
        given,
        66,
        2 * 4608 * 128 * 768,
        12 << 20,
    )
    got = exchange(sent)
    square = vmem((RES, RES), BF16)
    back = call(
        channel_kernel,
        [VMEM],
        shape((C, BACK_ROWS, C), BF16),
        HBM,
        [
            square,
            square,
            square,
            vmem((C, BACK_ROWS, C), BF16),
            dma((CHUNKS,)),
        ],
        [got],
        40,
        4 * RES**3,
        8 << 20,
    )
    returned = exchange(back)
    return call(
        back_kernel,
        [HBM] * 5,
        shape((ROWS, COLS, C), BF16),
        HBM,
        [
            vmem((GROUPS, C, BACK_STEP, C), BF16),
            vmem(saved.shape, BF16),
            vmem(inv.shape, F32),
            vmem(in_weight.shape, BF16),
            vmem(in_gain.shape, F32),
            vmem((BACK_SIZE, C), F32),
            vmem((C, C), F32),
            vmem((X_SIZE, C), F32),
            vmem((GROUPS, ROWS, GROUP, C), BF16),
            dma((GROUPS,)),
            dma((3 + GROUPS,)),
            dma((GROUPS,)),
        ],
        [returned, saved, inv, in_weight, in_gain],
        66,
        2 * 4608 * 128 * 640,
        12 << 20,
    )


def solution(mesh):
    return jax.shard_map(
        on_device,
        mesh=mesh,
        in_specs=(P("half", "ch", None),) * 3 + (P(),) * 9,
        out_specs=P("half", "ch", None),
        check_vma=False,
    )
```

```python
import jax
import jax.numpy as jnp
from jax import lax
from jax.experimental import pallas as pl
from jax.experimental.pallas import tpu as pltpu
from jax.sharding import PartitionSpec as P

EPSILON = 1e-05
AXES = ("ch", "half")
F32 = jnp.float32
BF16 = jnp.bfloat16

ROWS, COLS, C, RES = 192, 24, 128, 768
GROUP, PAIRS, GROUPS = 8, 4, 3
STEP, TAIL_AT, TAIL, OUT_ROWS = 32, 96, 16, 112
BACK_STEP, BACK_ROWS = 24, 72
X_PITCH, OUT_PITCH, TAIL_PITCH, BACK_PITCH = GROUP + 1, STEP + 1, TAIL + 1, BACK_STEP + 1
X_SIZE, OUT_SIZE, BACK_SIZE = ROWS * X_PITCH, C * OUT_PITCH, C * BACK_PITCH
FETCHES = 8
CHUNKS = 2
CHUNK = RES // CHUNKS


def dot(a, b):
    return jnp.dot(a, b, preferred_element_type=F32)


def mean(x):
    return jnp.sum(x, 0, keepdims=True) * (1.0 / C)


def centre(x):
    centred = x - mean(x)
    return centred, lax.rsqrt(mean(centred * centred) + EPSILON)


def column(row):
    return jnp.broadcast_to(row[...].reshape(1, C), (C, C)).T


def swap(x):
    return pltpu.roll(x, 64, 1)


def low_lanes(shape):
    return lax.broadcasted_iota(jnp.int32, shape, 1) < 64


def copies(sources, targets, sems):
    started = [pltpu.make_async_copy(s, t, sems.at[n]) for n, (s, t) in enumerate(zip(sources, targets))]
    for copy in started:
        copy.start()
    return started


def spread(tiles, x, group, wait):
    for n in range(3):
        wait(group, n)

        def body(i, _):
            values = tiles[group, n, pl.ds(pl.multiple_of(i * 16, 16), 16)].astype(F32)
            for m in range(16):
                x[n, pl.ds((i * 16 + m) * X_PITCH, GROUP), :] = values[m]
            return 0

        lax.fori_loop(0, ROWS // 16, body, 0, unroll=12)


def gather(x, n, q, part):
    if part < 2:
        return x[n, pl.ds(q + PAIRS * part, C, stride=X_PITCH), :].T
    base = C * X_PITCH + q
    return jnp.concatenate([x[n, pl.ds(base + PAIRS * m, 64, stride=X_PITCH), :] for m in range(2)], 0).T


def find_keep(mask_v, chain_v, pairs_v, keep):
    code = jnp.where(mask_v[...] > 0, chain_v[...], -1)
    code = jnp.broadcast_to(code.reshape(1, RES), (8, RES))
    rows = pltpu.roll(code, lax.rem(RES - lax.axis_index("half") * ROWS, RES), 1)[:1]
    cols = pltpu.roll(code, lax.rem(RES - lax.axis_index("ch") * COLS, RES), 1)[:1, :C]
    cols = jnp.broadcast_to(cols, (C, C)).astype(F32).T[:COLS]
    tail = rows[:, C : 2 * C]
    tail = jnp.where(low_lanes((1, C)), tail, swap(tail))
    pairs = pairs_v[...].astype(F32) * 0.5
    for n, rows_n in enumerate((rows[:, :C], tail)):
        out = jnp.zeros((COLS, C), F32)
        for d in range(4):
            across = jnp.zeros((1, C), F32)
            for c in range(4):
                across = jnp.where(rows_n == c, jnp.broadcast_to(pairs[c : c + 1, d : d + 1], (1, C)), across)
            out = jnp.where(cols == float(d), jnp.broadcast_to(across, (COLS, C)), out)
        keep[n] = out


def keep_of(keep, col, part):
    if part < 2:
        return keep[0, pl.ds(col + PAIRS * part, 1), :]
    return jnp.where(low_lanes((1, C)), keep[1, pl.ds(col, 1), :], keep[1, pl.ds(col + PAIRS, 1), :])


def prepare(given, buffers, wt, wot, cols, keep, sems):
    mask_v, chain_v, pairs_v, w_v, wo_v, *gains, tiles = buffers
    started = copies(given[3:], buffers[:-1], sems)

    def tile(group, n):
        at = pl.ds(pl.multiple_of(group * GROUP, GROUP), GROUP)
        return pltpu.make_async_copy(given[n].at[:, at], tiles.at[group, n], sems.at[9 + group * 3 + n])

    for group in range(GROUPS):
        for n in range(3):
            tile(group, n).start()
    for copy in started:
        copy.wait()
    for n in range(5):
        part = w_v[:, n * C : (n + 1) * C].astype(F32).T
        wt[n] = (part * 0.5 if n in (1, 3, 4) else part).astype(BF16)
    wot[...] = wo_v[...].astype(F32).T.astype(BF16)
    for n, g in enumerate(gains):
        cols[n] = column(g)
    cols[4] = cols[2] * 0.5
    find_keep(mask_v, chain_v, pairs_v, keep)

    return lambda group, n: tile(group, n).wait()


def front_kernel(*refs):
    given, out_ref = refs[:12], refs[12]
    *buffers, x, wt, wot, cols, keep, stage, stage_tail, packed, sems, out_sems = refs[13:]
    wo_v, tiles = buffers[4], buffers[-1]
    wait = prepare(given, buffers, wt, wot, cols, keep, sems)
    for r in range(4):
        stage_tail[pl.ds(12 + r, C, stride=TAIL_PITCH), :] = jnp.zeros((C, C), F32)

    def send(group):
        rows = pl.ds(pl.multiple_of(group * STEP, STEP), STEP)
        return pltpu.make_async_copy(packed.at[:, rows], out_ref.at[:, rows], out_sems.at[group])

    def body(group, _):
        spread(tiles, x, group, wait)
        for q in range(PAIRS):
            col = group * GROUP + q

            def put(row, value):
                stage[pl.ds(row, C, stride=OUT_PITCH), :] = value

            for part in range(3):
                centred, inv = centre(gather(x, 0, q, part))
                nz = (centred * inv * cols[0] + cols[1]).astype(BF16)
                kept = keep_of(keep, col, part)
                left = (jnp.tanh(dot(wt[1], nz)) + 1.0) * (dot(wt[0], nz) * kept)
                right = (jnp.tanh(dot(wt[3], nz)) + 1.0) * (dot(wt[2], nz) * kept)
                outer = ((jnp.tanh(dot(wt[4], nz)) + 1.0) * gather(x, 2, q, part)).astype(BF16)
                centred, inv = centre(gather(x, 1, q, part))
                h = dot(wo_v[...], outer) * cols[4]
                second = mean(h * centred) * (inv * inv)
                grad = inv * (h - mean(h) - centred * second)
                if part < 2:
                    put(q + PAIRS * part, grad)
                    put(GROUP + q + PAIRS * part, left)
                    put(2 * GROUP + q + PAIRS * part, right)
                else:
                    low = low_lanes((C, C))
                    stage_tail[pl.ds(group * PAIRS + q, C, stride=TAIL_PITCH), :] = grad
                    put(3 * GROUP + q, jnp.where(low, left, swap(right)))
                    put(3 * GROUP + PAIRS + q, jnp.where(low, swap(left), right))

        def pack(c, _):
            rows = pl.ds(pl.multiple_of(group * STEP, STEP), STEP)
            packed[c, rows] = stage[pl.ds(c * OUT_PITCH, STEP), :].astype(BF16)
            return 0

        for c in range(C):
            pack(c, 0)

        @pl.when(group < GROUPS - 1)
        def _():
            send(group).start()

        return 0

    lax.fori_loop(0, GROUPS, body, 0)

    def pack(c, _):
        packed[c, TAIL_AT:] = stage_tail[pl.ds(c * TAIL_PITCH, TAIL), :].astype(BF16)
        return 0

    for c in range(C):
        pack(c, 0)
    rest = pl.ds((GROUPS - 1) * STEP, OUT_ROWS - (GROUPS - 1) * STEP)
    final = pltpu.make_async_copy(packed.at[:, rest], out_ref.at[:, rest], out_sems.at[GROUPS - 1])
    final.start()
    for group in range(GROUPS - 1):
        send(group).wait()
    final.wait()


def save_kernel(*refs):
    given, saved_ref, inv_ref = refs[:12], refs[12], refs[13]
    *buffers, x, wt, wot, cols, keep, sems = refs[14:]
    tiles = buffers[-1]
    wait = prepare(given, buffers, wt, wot, cols, keep, sems)

    def body(group, _):
        spread(tiles, x, group, wait)

        def pair(q, _):
            n, col = group * PAIRS + q, group * GROUP + q
            for part in range(3):
                centred, inv = centre(gather(x, 0, q, part))
                unit_z = centred * inv
                nz = (unit_z * cols[0] + cols[1]).astype(BF16)
                kept_by = keep_of(keep, col, part)
                for m in (0, 1):
                    gate = jnp.tanh(dot(wt[2 * m + 1], nz))
                    kept = (gate + 1.0) * kept_by
                    saved_ref[n, part, 2 * m] = kept.astype(BF16)
                    saved_ref[n, part, 2 * m + 1] = (kept * dot(wt[2 * m], nz) * (0.5 - 0.5 * gate)).astype(BF16)
                gate = jnp.tanh(dot(wt[4], nz))
                centred, inv_x = centre(gather(x, 1, q, part))
                nx = (centred * inv_x * cols[2] + cols[3]).astype(BF16)
                slope = (0.5 + 0.5 * gate) * (0.5 - 0.5 * gate)
                saved_ref[n, part, 4] = (gather(x, 2, q, part) * dot(wot[...], nx) * slope).astype(BF16)
                saved_ref[n, part, 5] = unit_z.astype(BF16)
                inv_ref[n, part] = jnp.broadcast_to(inv, (8, C))
            return 0

        lax.fori_loop(0, PAIRS, pair, 0)
        return 0

    lax.fori_loop(0, GROUPS, body, 0)


def channel_kernel(in_v, out_ref, g, left, right, out_v, sems):
    low8, low16, low24 = (low_lanes((n, C)) for n in (GROUP, TAIL, COLS))

    def take(w):
        blocks = [in_v[w * 4 + h].astype(F32) for h in range(4)]

        def part(n):
            at = [STEP * m + GROUP * n for m in range(3)]
            return [jnp.concatenate([b[a : a + GROUP] for a in at], 0) for b in blocks]

        rows_g, rows_l, rows_r, mixed = part(0), part(1), part(2), part(3)
        for h in (0, 2):
            a, b = blocks[h][TAIL_AT:], blocks[h + 1][TAIL_AT:]
            one, two = jnp.where(low16, a, swap(b)), jnp.where(low16, swap(a), b)
            pieces = [v[PAIRS * m : PAIRS * (m + 1)] for m in range(3) for v in (one, two)]
            rows_g.append(jnp.concatenate(pieces, 0))
            a, b = mixed[h], mixed[h + 1]
            rows_l.append(jnp.where(low24, a, swap(b)))
            rows_r.append(jnp.where(low24, swap(a), b))
        return [jnp.concatenate(rows, 1) for rows in (rows_g, rows_l, rows_r)]

    def move(pair):
        one, two = take(2 * pair), take(2 * pair + 1)
        at = pl.ds(pl.multiple_of(pair * 48, 16), 48)
        both = [jnp.concatenate([a, b], 0).astype(BF16) for a, b in zip(one, two)]
        left[at, :] = both[1]
        right[at, :] = both[2]
        for n in range(3):
            block = pair * 3 + n
            half = block // 12
            rest = block - half * 12
            to = jnp.where(rest < 8, half * 8 + rest, 32 + half * 4 + rest - 8)
            g[pl.ds(pl.multiple_of(to * 16, 16), 16), :] = both[0][n * 16 : (n + 1) * 16]

    def body(n, _):
        for pair in range(16 // FETCHES):
            move(n * (16 // FETCHES) + pair)
        return 0

    lax.fori_loop(0, FETCHES, body, 0, unroll=2)

    def send(n):
        part = pl.ds(n * (C // CHUNKS), C // CHUNKS)
        return pltpu.make_async_copy(out_v.at[part], out_ref.at[part], sems.at[n])

    for n in range(CHUNKS):
        rows = slice(n * CHUNK, (n + 1) * CHUNK)
        back_l = dot(right[rows, :], g[...])
        back_r = lax.dot_general(left[rows, :], g[...], (((1,), (1,)), ((), ())), preferred_element_type=F32)
        for w in range(CHUNK // COLS):
            for h in range(4):
                lanes, tail = slice(h * C, (h + 1) * C), slice((4 + h // 2) * C, (5 + h // 2) * C)
                pieces = []
                for m in range(3):
                    at = slice(w * COLS + m * GROUP, w * COLS + (m + 1) * GROUP)
                    a, b = back_l[at, tail], back_r[at, tail]
                    mixed = jnp.where(low8, a, swap(b)) if h % 2 == 0 else jnp.where(low8, swap(a), b)
                    pieces += [back_l[at, lanes], back_r[at, lanes], mixed]
                out_v[(n * (CHUNK // COLS) + w) * 4 + h] = jnp.concatenate(pieces, 0).astype(BF16)
        send(n).start()
    for n in range(CHUNKS):
        send(n).wait()


def back_kernel(
    in_ref, saved_ref, inv_ref, w_ref, gain_ref, out_ref,
    in_v, saved_v, inv_v, w_v, gain_v, rows, cols, stage, out_v, in_sems, sems, out_sems,
):

    def fetch(n):
        at = pl.ds(pl.multiple_of(n * BACK_STEP, 8), BACK_STEP)
        return pltpu.make_async_copy(in_ref.at[:, at], in_v.at[n], in_sems.at[n])

    started = copies([w_ref, gain_ref, inv_ref], [w_v, gain_v, inv_v], sems)

    def take(group):
        at = pl.ds(group * PAIRS, PAIRS)
        return pltpu.make_async_copy(saved_ref.at[at], saved_v.at[at], sems.at[3 + group])

    for group in range(GROUPS):
        fetch(group).start()
        take(group).start()
    low = low_lanes((C, C))

    def send(group):
        at = pl.ds(pl.multiple_of(group * GROUP, GROUP), GROUP)
        return pltpu.make_async_copy(out_v.at[group], out_ref.at[:, at], out_sems.at[group])

    for copy in started:
        copy.wait()
    cols[...] = column(gain_v)

    def body(group, _):
        fetch(group).wait()

        def fill(c, _):
            rows[pl.ds(c * BACK_PITCH, BACK_STEP), :] = in_v[group, c].astype(F32)
            return 0

        for c in range(C):
            fill(c, 0)
        take(group).wait()

        def get(row):
            return rows[pl.ds(row, C, stride=BACK_PITCH), :]

        def put(row, value):
            stage[pl.ds(row, value.shape[0], stride=X_PITCH), :] = value

        for q in range(PAIRS):
            n = group * PAIRS + q
            a, b = get(2 * GROUP + q), get(2 * GROUP + PAIRS + q)
            lefts = [get(q), get(PAIRS + q), jnp.where(low, a, swap(b))]
            rights = [get(GROUP + q), get(GROUP + PAIRS + q), jnp.where(low, swap(a), b)]
            for part in range(3):
                saved = saved_v.at[n, part]
                grad_l, grad_r = lefts[part].astype(BF16), rights[part].astype(BF16)
                pieces = [grad_l * saved[0], grad_l * saved[1], grad_r * saved[2], grad_r * saved[3], saved[4]]
                e = dot(w_v[...], jnp.concatenate(pieces, 0)) * cols[...]
                unit_z = saved[5].astype(F32)
                grad = (inv_v[n, part][:1] * (e - mean(e) - unit_z * mean(e * unit_z))).T
                if part < 2:
                    put(q + PAIRS * part, grad)
                else:
                    put(C * X_PITCH + q, grad[:64])
                    put(C * X_PITCH + PAIRS + q, grad[64:])

        def flush(i, _):
            found = [stage[pl.ds((i * 16 + m) * X_PITCH, GROUP), :].reshape(1, GROUP, C) for m in range(16)]
            out_v[group, pl.ds(i * 16, 16)] = jnp.concatenate(found, 0).astype(BF16)
            return 0

        lax.fori_loop(0, ROWS // 16, flush, 0, unroll=12)
        send(group).start()
        return 0

    lax.fori_loop(0, GROUPS, body, 0)
    for group in range(GROUPS):
        send(group).wait()


HBM = pl.BlockSpec(memory_space=pltpu.HBM)
VMEM = pl.BlockSpec(memory_space=pltpu.VMEM)


def call(kernel, ins, outs, out_specs, scratch, args, limit, flops, moved):
    return pl.pallas_call(
        kernel,
        out_shape=outs,
        in_specs=ins,
        out_specs=out_specs,
        scratch_shapes=scratch,
        compiler_params=pltpu.CompilerParams(vmem_limit_bytes=limit << 20),
        cost_estimate=pl.CostEstimate(flops=flops, bytes_accessed=moved, transcendentals=0),
    )(*args)


def exchange(x):
    return lax.all_to_all(x, AXES, split_axis=0, concat_axis=0, tiled=True)


def on_device(*given):
    shape, vmem, dma = jax.ShapeDtypeStruct, pltpu.VMEM, pltpu.SemaphoreType.DMA
    in_weight, in_gain = given[6], given[8]
    buffers = [
        *(vmem(v.shape, v.dtype) for v in given[3:]),
        vmem((GROUPS, 3, ROWS, GROUP, C), BF16),
        vmem((3, X_SIZE, C), F32),
        vmem((5, C, C), BF16),
        vmem((C, C), BF16),
        vmem((5, C, C), F32),
        vmem((2, COLS, C), F32),
    ]
    sent = call(
        front_kernel,
        [HBM] * 12,
        shape((C, OUT_ROWS, C), BF16),
        HBM,
        [
            *buffers,
            vmem((OUT_SIZE, C), F32),
            vmem((C * TAIL_PITCH, C), F32),
            vmem((C, OUT_ROWS, C), BF16),
            dma((18,)),
            dma((GROUPS,)),
        ],
        given,
        66,
        2 * 4608 * 128 * 768,
        8 << 20,
    )
    saved, inv = call(
        save_kernel,
        [HBM] * 12,
        (shape((GROUPS * PAIRS, 3, 6, C, C), BF16), shape((GROUPS * PAIRS, 3, 8, C), F32)),
        (VMEM, VMEM),
        [*buffers, dma((18,))],
        given,
        66,
        2 * 4608 * 128 * 768,
        12 << 20,
    )
    got = exchange(sent)
    square = vmem((RES, RES), BF16)
    back = call(
        channel_kernel,
        [VMEM],
        shape((C, BACK_ROWS, C), BF16),
        HBM,
        [
            square,
            square,
            square,
            vmem((C, BACK_ROWS, C), BF16),
            dma((CHUNKS,)),
        ],
        [got],
        40,
        4 * RES**3,
        8 << 20,
    )
    returned = exchange(back)
    return call(
        back_kernel,
        [HBM] * 5,
        shape((ROWS, COLS, C), BF16),
        HBM,
        [
            vmem((GROUPS, C, BACK_STEP, C), BF16),
            vmem(saved.shape, BF16),
            vmem(inv.shape, F32),
            vmem(in_weight.shape, BF16),
            vmem(in_gain.shape, F32),
            vmem((BACK_SIZE, C), F32),
            vmem((C, C), F32),
            vmem((X_SIZE, C), F32),
            vmem((GROUPS, ROWS, GROUP, C), BF16),
            dma((GROUPS,)),
            dma((3 + GROUPS,)),
            dma((GROUPS,)),
        ],
        [returned, saved, inv, in_weight, in_gain],
        66,
        2 * 4608 * 128 * 640,
        12 << 20,
    )


def solution(mesh):
    return jax.shard_map(
        on_device,
        mesh=mesh,
        in_specs=(P("half", "ch", None),) * 3 + (P(),) * 9,
        out_specs=P("half", "ch", None),
        check_vma=False,
    )
```

```python
import jax
import jax.numpy as jnp
from jax import lax
from jax.experimental import pallas as pl
from jax.experimental.pallas import tpu as pltpu
from jax.sharding import PartitionSpec as P

EPSILON = 1e-05
AXES = ("ch", "half")
F32 = jnp.float32
BF16 = jnp.bfloat16

ROWS, COLS, C, RES = 192, 24, 128, 768
GROUP, PAIRS, GROUPS = 8, 4, 3
STEP, TAIL_AT, TAIL, OUT_ROWS = 32, 96, 16, 112
BACK_STEP, BACK_ROWS = 24, 72
X_PITCH, OUT_PITCH, TAIL_PITCH, BACK_PITCH = GROUP + 1, STEP + 1, TAIL + 1, BACK_STEP + 1
X_SIZE, OUT_SIZE, BACK_SIZE = ROWS * X_PITCH, C * OUT_PITCH, C * BACK_PITCH
FETCHES = 8
ENDS = 4
CHUNKS = 2
CHUNK = RES // CHUNKS
SENT = 4


def dot(a, b):
    return jnp.dot(a, b, preferred_element_type=F32)


def mean(x):
    return jnp.sum(x, 0, keepdims=True) * (1.0 / C)


def centre(x):
    centred = x - mean(x)
    return centred, lax.rsqrt(mean(centred * centred) + EPSILON)


def column(row):
    return jnp.broadcast_to(row[...].reshape(1, C), (C, C)).T


def swap(x):
    return pltpu.roll(x, 64, 1)


def low_lanes(shape):
    return lax.broadcasted_iota(jnp.int32, shape, 1) < 64


def copies(sources, targets, sems):
    started = [pltpu.make_async_copy(s, t, sems.at[n]) for n, (s, t) in enumerate(zip(sources, targets))]
    for copy in started:
        copy.start()
    return started


def spread(tiles, x, group, wait):
    for n in range(3):
        wait(group, n)

        def body(i, _):
            values = tiles[group, n, pl.ds(pl.multiple_of(i * 16, 16), 16)].astype(F32)
            for m in range(16):
                x[n, pl.ds((i * 16 + m) * X_PITCH, GROUP), :] = values[m]
            return 0

        lax.fori_loop(0, ROWS // 16, body, 0, unroll=12)


def gather(x, n, q, part):
    if part < 2:
        return x[n, pl.ds(q + PAIRS * part, C, stride=X_PITCH), :].T
    base = C * X_PITCH + q
    return jnp.concatenate([x[n, pl.ds(base + PAIRS * m, 64, stride=X_PITCH), :] for m in range(2)], 0).T


def find_keep(mask_v, chain_v, pairs_v, keep):
    code = jnp.where(mask_v[...] > 0, chain_v[...], -1)
    code = jnp.broadcast_to(code.reshape(1, RES), (8, RES))
    rows = pltpu.roll(code, lax.rem(RES - lax.axis_index("half") * ROWS, RES), 1)[:1]
    cols = pltpu.roll(code, lax.rem(RES - lax.axis_index("ch") * COLS, RES), 1)[:1, :C]
    cols = jnp.broadcast_to(cols, (C, C)).astype(F32).T[:COLS]
    tail = rows[:, C : 2 * C]
    tail = jnp.where(low_lanes((1, C)), tail, swap(tail))
    pairs = pairs_v[...].astype(F32) * 0.5
    for n, rows_n in enumerate((rows[:, :C], tail)):
        out = jnp.zeros((COLS, C), F32)
        for d in range(4):
            across = jnp.zeros((1, C), F32)
            for c in range(4):
                across = jnp.where(rows_n == c, jnp.broadcast_to(pairs[c : c + 1, d : d + 1], (1, C)), across)
            out = jnp.where(cols == float(d), jnp.broadcast_to(across, (COLS, C)), out)
        keep[n] = out


def keep_of(keep, col, part):
    if part < 2:
        return keep[0, pl.ds(col + PAIRS * part, 1), :]
    return jnp.where(low_lanes((1, C)), keep[1, pl.ds(col, 1), :], keep[1, pl.ds(col + PAIRS, 1), :])


def prepare(given, buffers, wt, wot, cols, keep, sems):
    mask_v, chain_v, pairs_v, w_v, wo_v, *gains, tiles = buffers
    started = copies(given[3:], buffers[:-1], sems)

    def tile(group, n):
        at = pl.ds(pl.multiple_of(group * GROUP, GROUP), GROUP)
        return pltpu.make_async_copy(given[n].at[:, at], tiles.at[group, n], sems.at[9 + group * 3 + n])

    for group in range(GROUPS):
        for n in range(3):
            tile(group, n).start()
    for copy in started:
        copy.wait()
    for n in range(5):
        part = w_v[:, n * C : (n + 1) * C].astype(F32).T
        wt[n] = (part * 0.5 if n in (1, 3, 4) else part).astype(BF16)
    for n, g in enumerate(gains[:3]):
        cols[n] = column(g)
    cols[4] = cols[2] * 0.5
    find_keep(mask_v, chain_v, pairs_v, keep)

    return lambda group, n: tile(group, n).wait()


def front_kernel(*refs):
    given, out_ref = refs[:12], refs[12]
    *buffers, x, wt, wot, cols, keep, stage, stage_tail, packed, sems, out_sems = refs[13:]
    wo_v, tiles = buffers[4], buffers[-1]
    wait = prepare(given, buffers, wt, wot, cols, keep, sems)
    for r in range(4):
        stage_tail[pl.ds(12 + r, C, stride=TAIL_PITCH), :] = jnp.zeros((C, C), F32)

    def send(group):
        rows = pl.ds(pl.multiple_of(group * STEP, STEP), STEP)
        return pltpu.make_async_copy(packed.at[:, rows], out_ref.at[:, rows], out_sems.at[group])

    def pack(c, group):
        rows = pl.ds(pl.multiple_of(group * STEP, STEP), STEP)
        packed[c, rows] = stage[pl.ds(c * OUT_PITCH, STEP), :].astype(BF16)

    def body(group, _):
        spread(tiles, x, group, wait)
        for q in range(PAIRS):
            col = group * GROUP + q

            def put(row, value):
                stage[pl.ds(row, C, stride=OUT_PITCH), :] = value

            for part in range(3):
                centred, inv = centre(gather(x, 0, q, part))
                nz = (centred * inv * cols[0] + cols[1]).astype(BF16)
                kept = keep_of(keep, col, part)
                left = (jnp.tanh(dot(wt[1], nz)) + 1.0) * (dot(wt[0], nz) * kept)
                right = (jnp.tanh(dot(wt[3], nz)) + 1.0) * (dot(wt[2], nz) * kept)
                outer = ((jnp.tanh(dot(wt[4], nz)) + 1.0) * gather(x, 2, q, part)).astype(BF16)
                centred, inv = centre(gather(x, 1, q, part))
                h = dot(wo_v[...], outer) * cols[4]
                second = mean(h * centred) * (inv * inv)
                grad = inv * (h - mean(h) - centred * second)
                if part < 2:
                    put(q + PAIRS * part, grad)
                    put(GROUP + q + PAIRS * part, left)
                    put(2 * GROUP + q + PAIRS * part, right)
                else:
                    low = low_lanes((C, C))
                    stage_tail[pl.ds(group * PAIRS + q, C, stride=TAIL_PITCH), :] = grad
                    put(3 * GROUP + q, jnp.where(low, left, swap(right)))
                    put(3 * GROUP + PAIRS + q, jnp.where(low, swap(left), right))

        @pl.when(group < GROUPS - 1)
        def _():
            for c in range(C):
                pack(c, group)
            send(group).start()

        return 0

    lax.fori_loop(0, GROUPS, body, 0)
    last = GROUPS - 1

    def send_last(n):
        part, rest = pl.ds(n * (C // ENDS), C // ENDS), pl.ds(last * STEP, OUT_ROWS - last * STEP)
        return pltpu.make_async_copy(packed.at[part, rest], out_ref.at[part, rest], out_sems.at[last + n])

    for c in range(C):
        pack(c, last)
        packed[c, TAIL_AT:] = stage_tail[pl.ds(c * TAIL_PITCH, TAIL), :].astype(BF16)
        if (c + 1) % (C // ENDS) == 0:
            send_last(c // (C // ENDS)).start()
    for group in range(last):
        send(group).wait()
    for n in range(ENDS):
        send_last(n).wait()


def save_kernel(*refs):
    given, saved_ref, inv_ref = refs[:12], refs[12], refs[13]
    *buffers, x, wt, wot, cols, keep, sems = refs[14:]
    tiles = buffers[-1]
    wait = prepare(given, buffers, wt, wot, cols, keep, sems)
    wot[...] = buffers[4][...].astype(F32).T.astype(BF16)
    cols[3] = column(buffers[8])

    def body(group, _):
        spread(tiles, x, group, wait)

        def pair(q, _):
            n, col = group * PAIRS + q, group * GROUP + q
            for part in range(3):
                centred, inv = centre(gather(x, 0, q, part))
                unit_z = centred * inv
                nz = (unit_z * cols[0] + cols[1]).astype(BF16)
                kept_by = keep_of(keep, col, part)
                for m in (0, 1):
                    gate = jnp.tanh(dot(wt[2 * m + 1], nz))
                    kept = (gate + 1.0) * kept_by
                    saved_ref[n, part, 2 * m] = kept.astype(BF16)
                    saved_ref[n, part, 2 * m + 1] = (kept * dot(wt[2 * m], nz) * (0.5 - 0.5 * gate)).astype(BF16)
                gate = jnp.tanh(dot(wt[4], nz))
                centred, inv_x = centre(gather(x, 1, q, part))
                nx = (centred * inv_x * cols[2] + cols[3]).astype(BF16)
                slope = (0.5 + 0.5 * gate) * (0.5 - 0.5 * gate)
                saved_ref[n, part, 4] = (gather(x, 2, q, part) * dot(wot[...], nx) * slope).astype(BF16)
                saved_ref[n, part, 5] = unit_z.astype(BF16)
                inv_ref[n, part] = jnp.broadcast_to(inv, (8, C))
            return 0

        lax.fori_loop(0, PAIRS, pair, 0)
        return 0

    lax.fori_loop(0, GROUPS, body, 0)


def channel_kernel(in_v, out_ref, g, left, right, out_v, sems):
    low8, low16, low24 = (low_lanes((n, C)) for n in (GROUP, TAIL, COLS))

    def take(w):
        blocks = [in_v[w * 4 + h].astype(F32) for h in range(4)]

        def part(n):
            at = [STEP * m + GROUP * n for m in range(3)]
            return [jnp.concatenate([b[a : a + GROUP] for a in at], 0) for b in blocks]

        rows_g, rows_l, rows_r, mixed = part(0), part(1), part(2), part(3)
        for h in (0, 2):
            a, b = blocks[h][TAIL_AT:], blocks[h + 1][TAIL_AT:]
            one, two = jnp.where(low16, a, swap(b)), jnp.where(low16, swap(a), b)
            pieces = [v[PAIRS * m : PAIRS * (m + 1)] for m in range(3) for v in (one, two)]
            rows_g.append(jnp.concatenate(pieces, 0))
            a, b = mixed[h], mixed[h + 1]
            rows_l.append(jnp.where(low24, a, swap(b)))
            rows_r.append(jnp.where(low24, swap(a), b))
        return [jnp.concatenate(rows, 1) for rows in (rows_g, rows_l, rows_r)]

    def move(pair):
        one, two = take(2 * pair), take(2 * pair + 1)
        at = pl.ds(pl.multiple_of(pair * 48, 16), 48)
        both = [jnp.concatenate([a, b], 0).astype(BF16) for a, b in zip(one, two)]
        left[at, :] = both[1]
        right[at, :] = both[2]
        for n in range(3):
            block = pair * 3 + n
            half = block // 12
            rest = block - half * 12
            to = jnp.where(rest < 8, half * 8 + rest, 32 + half * 4 + rest - 8)
            g[pl.ds(pl.multiple_of(to * 16, 16), 16), :] = both[0][n * 16 : (n + 1) * 16]

    def body(n, _):
        for pair in range(16 // FETCHES):
            move(n * (16 // FETCHES) + pair)
        return 0

    lax.fori_loop(0, FETCHES, body, 0, unroll=2)

    def send(n):
        part = pl.ds(n * 4 * SENT, 4 * SENT)
        return pltpu.make_async_copy(out_v.at[part], out_ref.at[part], sems.at[n])

    for n in range(CHUNKS):
        rows = slice(n * CHUNK, (n + 1) * CHUNK)
        back_l = dot(right[rows, :], g[...])
        back_r = lax.dot_general(left[rows, :], g[...], (((1,), (1,)), ((), ())), preferred_element_type=F32)
        for w in range(CHUNK // COLS):
            for h in range(4):
                lanes, tail = slice(h * C, (h + 1) * C), slice((4 + h // 2) * C, (5 + h // 2) * C)
                pieces = []
                for m in range(3):
                    at = slice(w * COLS + m * GROUP, w * COLS + (m + 1) * GROUP)
                    a, b = back_l[at, tail], back_r[at, tail]
                    mixed = jnp.where(low8, a, swap(b)) if h % 2 == 0 else jnp.where(low8, swap(a), b)
                    pieces += [back_l[at, lanes], back_r[at, lanes], mixed]
                out_v[(n * (CHUNK // COLS) + w) * 4 + h] = jnp.concatenate(pieces, 0).astype(BF16)
            if w % SENT == SENT - 1:
                send((n * (CHUNK // COLS) + w) // SENT).start()
    for n in range(32 // SENT):
        send(n).wait()


def back_kernel(
    in_ref, saved_ref, inv_ref, w_ref, gain_ref, out_ref,
    in_v, saved_v, inv_v, w_v, gain_v, rows, cols, stage, out_v, in_sems, sems, out_sems,
):

    def fetch(n):
        at = pl.ds(pl.multiple_of(n * BACK_STEP, 8), BACK_STEP)
        return pltpu.make_async_copy(in_ref.at[:, at], in_v.at[n], in_sems.at[n])

    started = copies([w_ref, gain_ref, inv_ref], [w_v, gain_v, inv_v], sems)

    def take(group):
        at = pl.ds(group * PAIRS, PAIRS)
        return pltpu.make_async_copy(saved_ref.at[at], saved_v.at[at], sems.at[3 + group])

    for group in range(GROUPS):
        fetch(group).start()
        take(group).start()
    low = low_lanes((C, C))

    def send(group):
        at = pl.ds(pl.multiple_of(group * GROUP, GROUP), GROUP)
        return pltpu.make_async_copy(out_v.at[group], out_ref.at[:, at], out_sems.at[group])

    for copy in started:
        copy.wait()
    cols[...] = column(gain_v)

    def body(group, _):
        fetch(group).wait()

        def fill(c, _):
            rows[pl.ds(c * BACK_PITCH, BACK_STEP), :] = in_v[group, c].astype(F32)
            return 0

        for c in range(C):
            fill(c, 0)
        take(group).wait()

        def get(row):
            return rows[pl.ds(row, C, stride=BACK_PITCH), :]

        def put(row, value):
            stage[pl.ds(row, value.shape[0], stride=X_PITCH), :] = value

        for q in range(PAIRS):
            n = group * PAIRS + q
            a, b = get(2 * GROUP + q), get(2 * GROUP + PAIRS + q)
            lefts = [get(q), get(PAIRS + q), jnp.where(low, a, swap(b))]
            rights = [get(GROUP + q), get(GROUP + PAIRS + q), jnp.where(low, swap(a), b)]
            for parts in ((0, 1), (2,)):

                def wide(take_one):
                    return jnp.concatenate([take_one(part) for part in parts], 1)

                grad_l = wide(lambda part: lefts[part].astype(BF16))
                grad_r = wide(lambda part: rights[part].astype(BF16))
                s0, s1, s2, s3, s4, s5 = (wide(lambda part, m=m: saved_v[n, part, m]) for m in range(6))
                pieces = [grad_l * s0, grad_l * s1, grad_r * s2, grad_r * s3, s4]
                e = dot(w_v[...], jnp.concatenate(pieces, 0)) * wide(lambda part: cols[...])
                unit_z = s5.astype(F32)
                inv = wide(lambda part: inv_v[n, part][:1])
                grad = (inv * (e - mean(e) - unit_z * mean(e * unit_z))).T
                if parts != (2,):
                    put(q, grad[:C])
                    put(q + PAIRS, grad[C:])
                else:
                    put(C * X_PITCH + q, grad[:64])
                    put(C * X_PITCH + PAIRS + q, grad[64:])

        def flush(i, _):
            found = [stage[pl.ds((i * 16 + m) * X_PITCH, GROUP), :].reshape(1, GROUP, C) for m in range(16)]
            out_v[group, pl.ds(i * 16, 16)] = jnp.concatenate(found, 0).astype(BF16)
            return 0

        lax.fori_loop(0, ROWS // 16, flush, 0, unroll=12)
        send(group).start()
        return 0

    lax.fori_loop(0, GROUPS, body, 0)
    for group in range(GROUPS):
        send(group).wait()


HBM = pl.BlockSpec(memory_space=pltpu.HBM)
VMEM = pl.BlockSpec(memory_space=pltpu.VMEM)


def call(kernel, ins, outs, out_specs, scratch, args, limit, flops, moved):
    return pl.pallas_call(
        kernel,
        out_shape=outs,
        in_specs=ins,
        out_specs=out_specs,
        scratch_shapes=scratch,
        compiler_params=pltpu.CompilerParams(vmem_limit_bytes=limit << 20),
        cost_estimate=pl.CostEstimate(flops=flops, bytes_accessed=moved, transcendentals=0),
    )(*args)


def exchange(x):
    return lax.all_to_all(x, AXES, split_axis=0, concat_axis=0, tiled=True)


def on_device(*given):
    shape, vmem, dma = jax.ShapeDtypeStruct, pltpu.VMEM, pltpu.SemaphoreType.DMA
    in_weight, in_gain = given[6], given[8]
    buffers = [
        *(vmem(v.shape, v.dtype) for v in given[3:]),
        vmem((GROUPS, 3, ROWS, GROUP, C), BF16),
        vmem((3, X_SIZE, C), F32),
        vmem((5, C, C), BF16),
        vmem((C, C), BF16),
        vmem((5, C, C), F32),
        vmem((2, COLS, C), F32),
    ]
    sent = call(
        front_kernel,
        [HBM] * 12,
        shape((C, OUT_ROWS, C), BF16),
        HBM,
        [
            *buffers,
            vmem((OUT_SIZE, C), F32),
            vmem((C * TAIL_PITCH, C), F32),
            vmem((C, OUT_ROWS, C), BF16),
            dma((18,)),
            dma((GROUPS - 1 + ENDS,)),
        ],
        given,
        66,
        2 * 4608 * 128 * 768,
        8 << 20,
    )
    saved, inv = call(
        save_kernel,
        [HBM] * 12,
        (shape((GROUPS * PAIRS, 3, 6, C, C), BF16), shape((GROUPS * PAIRS, 3, 8, C), F32)),
        (VMEM, VMEM),
        [*buffers, dma((18,))],
        given,
        66,
        2 * 4608 * 128 * 768,
        12 << 20,
    )
    got = exchange(sent)
    square = vmem((RES, RES), BF16)
    back = call(
        channel_kernel,
        [VMEM],
        shape((C, BACK_ROWS, C), BF16),
        HBM,
        [
            square,
            square,
            square,
            vmem((C, BACK_ROWS, C), BF16),
            dma((32 // SENT,)),
        ],
        [got],
        40,
        4 * RES**3,
        8 << 20,
    )
    returned = exchange(back)
    return call(
        back_kernel,
        [HBM] * 5,
        shape((ROWS, COLS, C), BF16),
        HBM,
        [
            vmem((GROUPS, C, BACK_STEP, C), BF16),
            vmem(saved.shape, BF16),
            vmem(inv.shape, F32),
            vmem(in_weight.shape, BF16),
            vmem(in_gain.shape, F32),
            vmem((BACK_SIZE, C), F32),
            vmem((C, C), F32),
            vmem((X_SIZE, C), F32),
            vmem((GROUPS, ROWS, GROUP, C), BF16),
            dma((GROUPS,)),
            dma((3 + GROUPS,)),
            dma((GROUPS,)),
        ],
        [returned, saved, inv, in_weight, in_gain],
        66,
        2 * 4608 * 128 * 640,
        12 << 20,
    )


def solution(mesh):
    return jax.shard_map(
        on_device,
        mesh=mesh,
        in_specs=(P("half", "ch", None),) * 3 + (P(),) * 9,
        out_specs=P("half", "ch", None),
        check_vma=False,
    )
```

```python
import jax
import jax.numpy as jnp
from jax import lax
from jax.experimental import pallas as pl
from jax.experimental.pallas import tpu as pltpu
from jax.sharding import PartitionSpec as P

EPSILON = 1e-05
AXES = ("ch", "half")
F32 = jnp.float32
BF16 = jnp.bfloat16

ROWS, COLS, C, RES = 192, 24, 128, 768
GROUP, PAIRS, GROUPS = 8, 4, 3
STEP, TAIL_AT, TAIL, OUT_ROWS = 32, 96, 16, 112
BACK_STEP, BACK_ROWS = 24, 72
X_PITCH, OUT_PITCH, TAIL_PITCH, BACK_PITCH = GROUP + 1, STEP + 1, TAIL + 1, BACK_STEP + 1
X_SIZE, OUT_SIZE, BACK_SIZE = ROWS * X_PITCH, C * OUT_PITCH, C * BACK_PITCH
FETCHES = 8
ENDS = 4
CHUNKS = 2
CHUNK = RES // CHUNKS
SENT = 4


def dot(a, b):
    return jnp.dot(a, b, preferred_element_type=F32)


def mean(x):
    return jnp.sum(x, 0, keepdims=True) * (1.0 / C)


def centre(x):
    centred = x - mean(x)
    return centred, lax.rsqrt(mean(centred * centred) + EPSILON)


def column(row):
    return jnp.broadcast_to(row[...].reshape(1, C), (C, C)).T


def swap(x):
    return pltpu.roll(x, 64, 1)


def low_lanes(shape):
    return lax.broadcasted_iota(jnp.int32, shape, 1) < 64


def copies(sources, targets, sems):
    started = [pltpu.make_async_copy(s, t, sems.at[n]) for n, (s, t) in enumerate(zip(sources, targets))]
    for copy in started:
        copy.start()
    return started


def spread(tiles, x, group, wait):
    for n in range(3):
        wait(group, n)

        def body(i, _):
            values = tiles[group, n, pl.ds(pl.multiple_of(i * 16, 16), 16)].astype(F32)
            for m in range(16):
                x[n, pl.ds((i * 16 + m) * X_PITCH, GROUP), :] = values[m]
            return 0

        lax.fori_loop(0, ROWS // 16, body, 0, unroll=12)


def gather(x, n, q, part):
    if part < 2:
        return x[n, pl.ds(q + PAIRS * part, C, stride=X_PITCH), :].T
    base = C * X_PITCH + q
    return jnp.concatenate([x[n, pl.ds(base + PAIRS * m, 64, stride=X_PITCH), :] for m in range(2)], 0).T


def find_keep(mask_v, chain_v, pairs_v, keep):
    code = jnp.where(mask_v[...] > 0, chain_v[...], -1)
    code = jnp.broadcast_to(code.reshape(1, RES), (8, RES))
    rows = pltpu.roll(code, lax.rem(RES - lax.axis_index("half") * ROWS, RES), 1)[:1]
    cols = pltpu.roll(code, lax.rem(RES - lax.axis_index("ch") * COLS, RES), 1)[:1, :C]
    cols = jnp.broadcast_to(cols, (C, C)).astype(F32).T[:COLS]
    tail = rows[:, C : 2 * C]
    tail = jnp.where(low_lanes((1, C)), tail, swap(tail))
    pairs = pairs_v[...].astype(F32) * 0.5
    for n, rows_n in enumerate((rows[:, :C], tail)):
        out = jnp.zeros((COLS, C), F32)
        for d in range(4):
            across = jnp.zeros((1, C), F32)
            for c in range(4):
                across = jnp.where(rows_n == c, jnp.broadcast_to(pairs[c : c + 1, d : d + 1], (1, C)), across)
            out = jnp.where(cols == float(d), jnp.broadcast_to(across, (COLS, C)), out)
        keep[n] = out


def keep_of(keep, col, part):
    if part < 2:
        return keep[0, pl.ds(col + PAIRS * part, 1), :]
    return jnp.where(low_lanes((1, C)), keep[1, pl.ds(col, 1), :], keep[1, pl.ds(col + PAIRS, 1), :])


def prepare(given, buffers, wt, wot, cols, keep, sems):
    mask_v, chain_v, pairs_v, w_v, wo_v, *gains, tiles = buffers
    started = copies(given[3:], buffers[:-1], sems)

    def tile(group, n):
        at = pl.ds(pl.multiple_of(group * GROUP, GROUP), GROUP)
        return pltpu.make_async_copy(given[n].at[:, at], tiles.at[group, n], sems.at[9 + group * 3 + n])

    for group in range(GROUPS):
        for n in range(3):
            tile(group, n).start()
    for copy in started:
        copy.wait()
    for n in range(5):
        part = w_v[:, n * C : (n + 1) * C].astype(F32).T
        wt[n] = (part * 0.5 if n in (1, 3, 4) else part).astype(BF16)
    wot[...] = wo_v[...].astype(F32).T.astype(BF16)
    for n, g in enumerate(gains):
        cols[n] = column(g)
    cols[4] = cols[2] * 0.5
    find_keep(mask_v, chain_v, pairs_v, keep)

    return lambda group, n: tile(group, n).wait()


def front_kernel(*refs):
    given, out_ref = refs[:12], refs[12]
    *buffers, x, wt, wot, cols, keep, stage, stage_tail, packed, sems, out_sems = refs[13:]
    wo_v, tiles = buffers[4], buffers[-1]
    wait = prepare(given, buffers, wt, wot, cols, keep, sems)
    for r in range(4):
        stage_tail[pl.ds(12 + r, C, stride=TAIL_PITCH), :] = jnp.zeros((C, C), F32)

    def send(group):
        rows = pl.ds(pl.multiple_of(group * STEP, STEP), STEP)
        return pltpu.make_async_copy(packed.at[:, rows], out_ref.at[:, rows], out_sems.at[group])

    def pack(c, group):
        rows = pl.ds(pl.multiple_of(group * STEP, STEP), STEP)
        packed[c, rows] = stage[pl.ds(c * OUT_PITCH, STEP), :].astype(BF16)

    def body(group, _):
        spread(tiles, x, group, wait)
        for q in range(PAIRS):
            col = group * GROUP + q

            def put(row, value):
                stage[pl.ds(row, C, stride=OUT_PITCH), :] = value

            for part in range(3):
                centred, inv = centre(gather(x, 0, q, part))
                nz = (centred * inv * cols[0] + cols[1]).astype(BF16)
                kept = keep_of(keep, col, part)
                left = (jnp.tanh(dot(wt[1], nz)) + 1.0) * (dot(wt[0], nz) * kept)
                right = (jnp.tanh(dot(wt[3], nz)) + 1.0) * (dot(wt[2], nz) * kept)
                outer = ((jnp.tanh(dot(wt[4], nz)) + 1.0) * gather(x, 2, q, part)).astype(BF16)
                centred, inv = centre(gather(x, 1, q, part))
                h = dot(wo_v[...], outer) * cols[4]
                second = mean(h * centred) * (inv * inv)
                grad = inv * (h - mean(h) - centred * second)
                if part < 2:
                    put(q + PAIRS * part, grad)
                    put(GROUP + q + PAIRS * part, left)
                    put(2 * GROUP + q + PAIRS * part, right)
                else:
                    low = low_lanes((C, C))
                    stage_tail[pl.ds(group * PAIRS + q, C, stride=TAIL_PITCH), :] = grad
                    put(3 * GROUP + q, jnp.where(low, left, swap(right)))
                    put(3 * GROUP + PAIRS + q, jnp.where(low, swap(left), right))

        @pl.when(group < GROUPS - 1)
        def _():
            for c in range(C):
                pack(c, group)
            send(group).start()

        return 0

    lax.fori_loop(0, GROUPS, body, 0)
    last = GROUPS - 1

    def send_last(n):
        part, rest = pl.ds(n * (C // ENDS), C // ENDS), pl.ds(last * STEP, OUT_ROWS - last * STEP)
        return pltpu.make_async_copy(packed.at[part, rest], out_ref.at[part, rest], out_sems.at[last + n])

    for c in range(C):
        pack(c, last)
        packed[c, TAIL_AT:] = stage_tail[pl.ds(c * TAIL_PITCH, TAIL), :].astype(BF16)
        if (c + 1) % (C // ENDS) == 0:
            send_last(c // (C // ENDS)).start()
    for group in range(last):
        send(group).wait()
    for n in range(ENDS):
        send_last(n).wait()


def save_kernel(*refs):
    given, saved_ref, inv_ref = refs[:12], refs[12], refs[13]
    *buffers, x, wt, wot, cols, keep, sems = refs[14:]
    tiles = buffers[-1]
    wait = prepare(given, buffers, wt, wot, cols, keep, sems)

    def body(group, _):
        spread(tiles, x, group, wait)

        def pair(q, _):
            n, col = group * PAIRS + q, group * GROUP + q
            for part in range(3):
                centred, inv = centre(gather(x, 0, q, part))
                unit_z = centred * inv
                nz = (unit_z * cols[0] + cols[1]).astype(BF16)
                kept_by = keep_of(keep, col, part)
                for m in (0, 1):
                    gate = jnp.tanh(dot(wt[2 * m + 1], nz))
                    kept = (gate + 1.0) * kept_by
                    saved_ref[n, part, 2 * m] = kept.astype(BF16)
                    saved_ref[n, part, 2 * m + 1] = (kept * dot(wt[2 * m], nz) * (0.5 - 0.5 * gate)).astype(BF16)
                gate = jnp.tanh(dot(wt[4], nz))
                centred, inv_x = centre(gather(x, 1, q, part))
                nx = (centred * inv_x * cols[2] + cols[3]).astype(BF16)
                slope = (0.5 + 0.5 * gate) * (0.5 - 0.5 * gate)
                saved_ref[n, part, 4] = (gather(x, 2, q, part) * dot(wot[...], nx) * slope).astype(BF16)
                saved_ref[n, part, 5] = unit_z.astype(BF16)
                inv_ref[n, part] = jnp.broadcast_to(inv, (8, C))
            return 0

        lax.fori_loop(0, PAIRS, pair, 0)
        return 0

    lax.fori_loop(0, GROUPS, body, 0)


def channel_kernel(in_v, out_ref, g, left, right, out_v, sems):
    low8, low16, low24 = (low_lanes((n, C)) for n in (GROUP, TAIL, COLS))

    def take(w):
        blocks = [in_v[w * 4 + h].astype(F32) for h in range(4)]

        def part(n):
            at = [STEP * m + GROUP * n for m in range(3)]
            return [jnp.concatenate([b[a : a + GROUP] for a in at], 0) for b in blocks]

        rows_g, rows_l, rows_r, mixed = part(0), part(1), part(2), part(3)
        for h in (0, 2):
            a, b = blocks[h][TAIL_AT:], blocks[h + 1][TAIL_AT:]
            one, two = jnp.where(low16, a, swap(b)), jnp.where(low16, swap(a), b)
            pieces = [v[PAIRS * m : PAIRS * (m + 1)] for m in range(3) for v in (one, two)]
            rows_g.append(jnp.concatenate(pieces, 0))
            a, b = mixed[h], mixed[h + 1]
            rows_l.append(jnp.where(low24, a, swap(b)))
            rows_r.append(jnp.where(low24, swap(a), b))
        return [jnp.concatenate(rows, 1) for rows in (rows_g, rows_l, rows_r)]

    def move(pair):
        one, two = take(2 * pair), take(2 * pair + 1)
        at = pl.ds(pl.multiple_of(pair * 48, 16), 48)
        both = [jnp.concatenate([a, b], 0).astype(BF16) for a, b in zip(one, two)]
        left[at, :] = both[1]
        right[at, :] = both[2]
        for n in range(3):
            block = pair * 3 + n
            half = block // 12
            rest = block - half * 12
            to = jnp.where(rest < 8, half * 8 + rest, 32 + half * 4 + rest - 8)
            g[pl.ds(pl.multiple_of(to * 16, 16), 16), :] = both[0][n * 16 : (n + 1) * 16]

    def body(n, _):
        for pair in range(16 // FETCHES):
            move(n * (16 // FETCHES) + pair)
        return 0

    lax.fori_loop(0, FETCHES, body, 0, unroll=2)

    def send(n):
        part = pl.ds(n * 4 * SENT, 4 * SENT)
        return pltpu.make_async_copy(out_v.at[part], out_ref.at[part], sems.at[n])

    for n in range(CHUNKS):
        rows = slice(n * CHUNK, (n + 1) * CHUNK)
        back_l = dot(right[rows, :], g[...])
        back_r = lax.dot_general(left[rows, :], g[...], (((1,), (1,)), ((), ())), preferred_element_type=F32)
        for w in range(CHUNK // COLS):
            for h in range(4):
                lanes, tail = slice(h * C, (h + 1) * C), slice((4 + h // 2) * C, (5 + h // 2) * C)
                pieces = []
                for m in range(3):
                    at = slice(w * COLS + m * GROUP, w * COLS + (m + 1) * GROUP)
                    a, b = back_l[at, tail], back_r[at, tail]
                    mixed = jnp.where(low8, a, swap(b)) if h % 2 == 0 else jnp.where(low8, swap(a), b)
                    pieces += [back_l[at, lanes], back_r[at, lanes], mixed]
                out_v[(n * (CHUNK // COLS) + w) * 4 + h] = jnp.concatenate(pieces, 0).astype(BF16)
            if w % SENT == SENT - 1:
                send((n * (CHUNK // COLS) + w) // SENT).start()
    for n in range(32 // SENT):
        send(n).wait()


def back_kernel(
    in_ref, saved_ref, inv_ref, w_ref, gain_ref, out_ref,
    in_v, saved_v, inv_v, w_v, gain_v, rows, cols, stage, out_v, in_sems, sems, out_sems,
):

    def fetch(n):
        at = pl.ds(pl.multiple_of(n * BACK_STEP, 8), BACK_STEP)
        return pltpu.make_async_copy(in_ref.at[:, at], in_v.at[n], in_sems.at[n])

    started = copies([w_ref, gain_ref, inv_ref], [w_v, gain_v, inv_v], sems)

    def take(group):
        at = pl.ds(group * PAIRS, PAIRS)
        return pltpu.make_async_copy(saved_ref.at[at], saved_v.at[at], sems.at[3 + group])

    for group in range(GROUPS):
        fetch(group).start()
        take(group).start()
    low = low_lanes((C, C))

    def send(group):
        at = pl.ds(pl.multiple_of(group * GROUP, GROUP), GROUP)
        return pltpu.make_async_copy(out_v.at[group], out_ref.at[:, at], out_sems.at[group])

    for copy in started:
        copy.wait()
    cols[...] = column(gain_v)

    def body(group, _):
        fetch(group).wait()

        def fill(c, _):
            rows[pl.ds(c * BACK_PITCH, BACK_STEP), :] = in_v[group, c].astype(F32)
            return 0

        for c in range(C):
            fill(c, 0)
        take(group).wait()

        def get(row):
            return rows[pl.ds(row, C, stride=BACK_PITCH), :]

        def put(row, value):
            stage[pl.ds(row, value.shape[0], stride=X_PITCH), :] = value

        for q in range(PAIRS):
            n = group * PAIRS + q
            a, b = get(2 * GROUP + q), get(2 * GROUP + PAIRS + q)
            lefts = [get(q), get(PAIRS + q), jnp.where(low, a, swap(b))]
            rights = [get(GROUP + q), get(GROUP + PAIRS + q), jnp.where(low, swap(a), b)]
            for part in range(3):
                saved = saved_v.at[n, part]
                grad_l, grad_r = lefts[part].astype(BF16), rights[part].astype(BF16)
                pieces = [grad_l * saved[0], grad_l * saved[1], grad_r * saved[2], grad_r * saved[3], saved[4]]
                e = dot(w_v[...], jnp.concatenate(pieces, 0)) * cols[...]
                unit_z = saved[5].astype(F32)
                grad = (inv_v[n, part][:1] * (e - mean(e) - unit_z * mean(e * unit_z))).T
                if part < 2:
                    put(q + PAIRS * part, grad)
                else:
                    put(C * X_PITCH + q, grad[:64])
                    put(C * X_PITCH + PAIRS + q, grad[64:])

        def flush(i, _):
            found = [stage[pl.ds((i * 16 + m) * X_PITCH, GROUP), :].reshape(1, GROUP, C) for m in range(16)]
            out_v[group, pl.ds(i * 16, 16)] = jnp.concatenate(found, 0).astype(BF16)
            return 0

        lax.fori_loop(0, ROWS // 16, flush, 0, unroll=12)
        send(group).start()
        return 0

    lax.fori_loop(0, GROUPS, body, 0)
    for group in range(GROUPS):
        send(group).wait()


HBM = pl.BlockSpec(memory_space=pltpu.HBM)
VMEM = pl.BlockSpec(memory_space=pltpu.VMEM)


def call(kernel, ins, outs, out_specs, scratch, args, limit, flops, moved):
    return pl.pallas_call(
        kernel,
        out_shape=outs,
        in_specs=ins,
        out_specs=out_specs,
        scratch_shapes=scratch,
        compiler_params=pltpu.CompilerParams(vmem_limit_bytes=limit << 20),
        cost_estimate=pl.CostEstimate(flops=flops, bytes_accessed=moved, transcendentals=0),
    )(*args)


def exchange(x):
    return lax.all_to_all(x, AXES, split_axis=0, concat_axis=0, tiled=True)


def on_device(*given):
    shape, vmem, dma = jax.ShapeDtypeStruct, pltpu.VMEM, pltpu.SemaphoreType.DMA
    in_weight, in_gain = given[6], given[8]
    buffers = [
        *(vmem(v.shape, v.dtype) for v in given[3:]),
        vmem((GROUPS, 3, ROWS, GROUP, C), BF16),
        vmem((3, X_SIZE, C), F32),
        vmem((5, C, C), BF16),
        vmem((C, C), BF16),
        vmem((5, C, C), F32),
        vmem((2, COLS, C), F32),
    ]
    sent = call(
        front_kernel,
        [HBM] * 12,
        shape((C, OUT_ROWS, C), BF16),
        HBM,
        [
            *buffers,
            vmem((OUT_SIZE, C), F32),
            vmem((C * TAIL_PITCH, C), F32),
            vmem((C, OUT_ROWS, C), BF16),
            dma((18,)),
            dma((GROUPS - 1 + ENDS,)),
        ],
        given,
        66,
        2 * 4608 * 128 * 768,
        8 << 20,
    )
    saved, inv = call(
        save_kernel,
        [HBM] * 12,
        (shape((GROUPS * PAIRS, 3, 6, C, C), BF16), shape((GROUPS * PAIRS, 3, 8, C), F32)),
        (VMEM, VMEM),
        [*buffers, dma((18,))],
        given,
        66,
        2 * 4608 * 128 * 768,
        12 << 20,
    )
    got = exchange(sent)
    square = vmem((RES, RES), BF16)
    back = call(
        channel_kernel,
        [VMEM],
        shape((C, BACK_ROWS, C), BF16),
        HBM,
        [
            square,
            square,
            square,
            vmem((C, BACK_ROWS, C), BF16),
            dma((32 // SENT,)),
        ],
        [got],
        40,
        4 * RES**3,
        8 << 20,
    )
    returned = exchange(back)
    return call(
        back_kernel,
        [HBM] * 5,
        shape((ROWS, COLS, C), BF16),
        HBM,
        [
            vmem((GROUPS, C, BACK_STEP, C), BF16),
            vmem(saved.shape, BF16),
            vmem(inv.shape, F32),
            vmem(in_weight.shape, BF16),
            vmem(in_gain.shape, F32),
            vmem((BACK_SIZE, C), F32),
            vmem((C, C), F32),
            vmem((X_SIZE, C), F32),
            vmem((GROUPS, ROWS, GROUP, C), BF16),
            dma((GROUPS,)),
            dma((3 + GROUPS,)),
            dma((GROUPS,)),
        ],
        [returned, saved, inv, in_weight, in_gain],
        66,
        2 * 4608 * 128 * 640,
        12 << 20,
    )


def solution(mesh):
    return jax.shard_map(
        on_device,
        mesh=mesh,
        in_specs=(P("half", "ch", None),) * 3 + (P(),) * 9,
        out_specs=P("half", "ch", None),
        check_vma=False,
    )
```
